512 devices in a mesh: gx: 4 (over y), gy: 8 (over x, core), gz: 16 (over z).
Axes of the slice: x: 4, y: 4, z: 16, core: 2. Of those that a mesh axis runs over, the one named last changes fastest.
Arguments:
- right_side: float32 [64, 256, 2048], P('gx', 'gy', 'gz'), may hold values from -24 to 24
- face_x: float32 [64, 256, 2048], P('gx', 'gy', 'gz'), may hold values from 0.2 to 5
- face_y: float32 [64, 256, 2048], P('gx', 'gy', 'gz'), may hold values from 0.2 to 5
- face_z: float32 [64, 256, 2048], P('gx', 'gy', 'gz'), may hold values from 0.2 to 5
- absorb: float32 [64, 256, 2048], P('gx', 'gy', 'gz'), may hold values from 0.02 to 0.2
Outputs:
- solution: float32 [64, 256, 2048], P('gx', 'gy', 'gz')
The draws below stay inside these ranges and needn't reach their ends.
All inputs are finite; a program needn't handle non-finite values.
Results may differ from the reference program's by a relative error of at most 0.00002.
Values sent between devices are 32-bit elements; how exact they have to be, the bound alone decides.
A program may use at most 64 MiB of HBM per device.

```python
import math
import jax
import jax.numpy as jnp
from jax import lax

SMOOTH = 2
COARSE_STEPS = 6
NX = 64
NY = 256
NZ = 2048


def block_scale(rng, shape, pieces, smallest, high):
    gain, own = 1.0, jax.random.fold_in(rng, 6)
    for position, parts in pieces:
        draws = jnp.exp(jax.random.uniform(jax.random.fold_in(own, position), (parts,), jnp.float32, smallest / len(pieces), high / len(pieces)))
        gain = gain * jnp.repeat(draws, shape[position] // parts).reshape([-1 if axis == position else 1 for axis in range(len(shape))])
    return gain


def bell_draw(rng, extent, spread, bound, shards=(), kind=jnp.bfloat16):
    loudness = block_scale(rng, extent, shards, -0.22, 0.18) if shards else 1.0
    drawn = jax.random.normal(rng, extent, jnp.float32) * spread * loudness
    return jnp.minimum(jnp.maximum(drawn, -bound), bound).astype(kind)


def setup_inputs(seed: int = 0) -> dict:
    splits = jax.random.split(jax.random.key(seed), 6)
    right_side = bell_draw(splits[0], (NX, NY, NZ), 4.0, 24.0, ((0, 4), (1, 8), (2, 16)), jnp.float32)
    face_x = jnp.clip(jnp.exp(math.log(5.0) - 3.218876 * jax.random.uniform(splits[1], (NX, NY, NZ), jnp.float32) ** block_scale(splits[1], (NX, NY, NZ), ((0, 4), (1, 8), (2, 16)), -0.2, 0.2)), 0.2, 5.0)
    face_y = jnp.clip(jnp.exp(math.log(5.0) - 3.218876 * jax.random.uniform(splits[2], (NX, NY, NZ), jnp.float32) ** block_scale(splits[2], (NX, NY, NZ), ((0, 4), (1, 8), (2, 16)), -0.2, 0.2)), 0.2, 5.0)
    face_z = jnp.clip(jnp.exp(math.log(5.0) - 3.218876 * jax.random.uniform(splits[3], (NX, NY, NZ), jnp.float32) ** block_scale(splits[3], (NX, NY, NZ), ((0, 4), (1, 8), (2, 16)), -0.2, 0.2)), 0.2, 5.0)
    absorb = jnp.clip(jnp.exp(math.log(0.2) - 2.3025851 * jax.random.uniform(splits[4], (NX, NY, NZ), jnp.float32) ** block_scale(splits[4], (NX, NY, NZ), ((0, 4), (1, 8), (2, 16)), -0.2, 0.2)), 0.02, 0.2)
    return dict(right_side=right_side, face_x=face_x, face_y=face_y, face_z=face_z, absorb=absorb)


smooth_lowest = 0.5
coarse_lowest = 0.05
upper_bound = 2.0


def zero_rim(field):
    return jnp.pad(field, 1)


def pair_mean(values, along):
    old_shape = values.shape
    new_shape = old_shape[:along] + (old_shape[along] // 2, 2) + old_shape[along + 1:]
    return jnp.sum(values.reshape(new_shape), axis=along + 1) * 0.5


def coarsen(face_x, face_y, face_z, absorb):
    coarse_x = 0.25 * pair_mean(pair_mean(face_x[1::2], 1), 2)
    coarse_y = 0.25 * pair_mean(pair_mean(face_y[:, 1::2], 0), 2)
    coarse_z = 0.25 * pair_mean(pair_mean(face_z[:, :, 1::2], 0), 1)
    coarse_abs = pair_mean(pair_mean(pair_mean(absorb, 0), 1), 2)
    return coarse_x, coarse_y, coarse_z, coarse_abs


def make_level(padded_x, padded_y, padded_z, absorb, padder):
    own_x = padded_x[1:-1, 1:-1, 1:-1]
    low_x = padded_x[:-2, 1:-1, 1:-1]
    own_y = padded_y[1:-1, 1:-1, 1:-1]
    low_y = padded_y[1:-1, :-2, 1:-1]
    own_z = padded_z[1:-1, 1:-1, 1:-1]
    low_z = padded_z[1:-1, 1:-1, :-2]
    diagonal = absorb + own_x + low_x + own_y + low_y + own_z + low_z

    def operate(field):
        padded = padder(field)
        centre = padded[1:-1, 1:-1, 1:-1]
        result = absorb * centre + own_x * (centre - padded[2:, 1:-1, 1:-1]) + low_x * (centre - padded[:-2, 1:-1, 1:-1])
        result = result + own_y * (centre - padded[1:-1, 2:, 1:-1]) + low_y * (centre - padded[1:-1, :-2, 1:-1])
        result = result + own_z * (centre - padded[1:-1, 1:-1, 2:]) + low_z * (centre - padded[1:-1, 1:-1, :-2])
        return result

    return operate, 1.0 / diagonal


def chebyshev(source, iterate, sweeps, lowest, highest, operate, inverse_diag):
    centre = 0.5 * (lowest + highest)
    half_width = 0.5 * (highest - lowest)
    sigma_one = centre / half_width
    factor = 1.0 / sigma_one
    if iterate is None:
        residual = source
        iterate = jnp.zeros_like(source)
    else:
        residual = source - operate(iterate)
    update = inverse_diag * residual / centre
    for _ in range(sweeps - 1):
        iterate = iterate + update
        residual = source - operate(iterate)
        factor_next = 1.0 / (2.0 * sigma_one - factor)
        update = factor_next * factor * update + (2.0 * factor_next / half_width) * inverse_diag * residual
        factor = factor_next
    return iterate + update


def restrict_axis(padded, along):
    length = padded.shape[along] - 2
    before = lax.slice_in_dim(padded, 0, length, 2, along)
    at_even = lax.slice_in_dim(padded, 1, length + 1, 2, along)
    at_odd = lax.slice_in_dim(padded, 2, length + 2, 2, along)
    after_two = lax.slice_in_dim(padded, 3, length + 2, 2, along)
    return (before + 3.0 * at_even + 3.0 * at_odd + after_two) * 0.125


def restrict(padded):
    for along in range(3):
        padded = restrict_axis(padded, along)
    return padded


def prolong_axis(padded, along):
    count = padded.shape[along] - 2
    centred = lax.slice_in_dim(padded, 1, count + 1, 1, along)
    lower_side = lax.slice_in_dim(padded, 0, count, 1, along)
    upper_side = lax.slice_in_dim(padded, 2, count + 2, 1, along)
    at_even = 0.75 * centred + 0.25 * lower_side
    at_odd = 0.75 * centred + 0.25 * upper_side
    paired = jnp.stack([at_even, at_odd], along + 1)
    new_shape = padded.shape[:along] + (2 * count,) + paired.shape[along + 2:]
    return paired.reshape(new_shape)


def prolong(padded):
    for along in range(3):
        padded = prolong_axis(padded, along)
    return padded


def reference(right_side, face_x, face_y, face_z, absorb):
    face_x = face_x.at[-1].set(0.0)
    face_y = face_y.at[:, -1].set(0.0)
    face_z = face_z.at[:, :, -1].set(0.0)
    operate_fine, inverse_fine = make_level(zero_rim(face_x), zero_rim(face_y), zero_rim(face_z), absorb, zero_rim)
    mid_x, mid_y, mid_z, mid_abs = coarsen(face_x, face_y, face_z, absorb)
    operate_mid, inverse_mid = make_level(zero_rim(mid_x), zero_rim(mid_y), zero_rim(mid_z), mid_abs, zero_rim)
    low_x, low_y, low_z, low_abs = coarsen(mid_x, mid_y, mid_z, mid_abs)
    operate_low, inverse_low = make_level(zero_rim(low_x), zero_rim(low_y), zero_rim(low_z), low_abs, zero_rim)

    fine_sol = chebyshev(right_side, None, SMOOTH, smooth_lowest, upper_bound, operate_fine, inverse_fine)
    mid_source = restrict(zero_rim(right_side - operate_fine(fine_sol)))
    mid_sol = chebyshev(mid_source, None, SMOOTH, smooth_lowest, upper_bound, operate_mid, inverse_mid)
    low_source = restrict(zero_rim(mid_source - operate_mid(mid_sol)))
    low_sol = chebyshev(low_source, None, COARSE_STEPS, coarse_lowest, upper_bound, operate_low, inverse_low)
    mid_sol = mid_sol + prolong(zero_rim(low_sol))
    mid_sol = chebyshev(mid_source, mid_sol, SMOOTH, smooth_lowest, upper_bound, operate_mid, inverse_mid)
    fine_sol = fine_sol + prolong(zero_rim(mid_sol))
    return chebyshev(right_side, fine_sol, SMOOTH, smooth_lowest, upper_bound, operate_fine, inverse_fine)
```

```python
import functools

import jax
import jax.numpy as jnp
from jax import lax
from jax.experimental import pallas as pl
from jax.experimental.pallas import tpu as pltpu
from jax.sharding import PartitionSpec as P

MESH = pl.DeviceIdType.MESH
F32 = jnp.float32
HI = lax.Precision.HIGHEST

B, S, FY, FZ, FX = range(5)

ALL26 = sorted(
    [(a, b, c) for a in (-1, 0, 1) for b in (-1, 0, 1) for c in (-1, 0, 1) if (a, b, c) != (0, 0, 0)],
    key=lambda d: -sum(map(abs, d)),
)


def cheb_factors(steps, lowest, highest):
    centre = 0.5 * (lowest + highest)
    half = 0.5 * (highest - lowest)
    q = centre / half
    rho = 1.0 / q
    out = []
    for _ in range(steps - 1):
        nxt = 1.0 / (2.0 * q - rho)
        out.append((nxt * rho, 2.0 * nxt / half))
        rho = nxt
    return 1.0 / centre, out


def iota(shape, dim):
    return lax.broadcasted_iota(jnp.int32, shape, dim)


def dot(a, b):
    return jnp.dot(a, b, precision=HI, preferred_element_type=F32)


def shift(v, amount, axis):
    return pltpu.roll(v, amount % v.shape[axis], axis)


def restrict_weights(z, k, ok):
    t = z - 2 * k
    w = jnp.where((t == 0) | (t == 1), 0.375, jnp.where((t == -1) | (t == 2), 0.125, 0.0))
    return jnp.where(ok, w, 0.0)


def prolong_weights(coarse, fine):
    k = fine >> 1
    side = jnp.where((fine & 1) == 0, k - 1, k + 1)
    return jnp.where(coarse == k, 0.75, jnp.where(coarse == side, 0.25, 0.0))


def kernel(sizes, b_in, fx_in, fy_in, fz_in, s_in, out,
           C, ID, V, D, W, RX, ZC, LC, ZV, LV,
           KP, K1, ZK, LK, B1, I1, X1, D1, T1, ZB, LB, RX1,
           K2P, LK2, B2P, LB2, K2, I2, X2, D2, Y2, PY1, PY0,
           in_sem, c_s, c_r, v_s, v_r, k_s, k_r, b_s, b_r, k2_s, k2_r, b2_s, b2_r):
    GX, GY, GZ = sizes
    gx, gy, gz = (lax.axis_index(a) for a in ("gx", "gy", "gz"))
    me = (gx, gy, gz)

    def dev(d):
        return tuple(lax.rem(m + (q + s), s) for m, q, s in zip(me, d, sizes))

    loads = []
    for f, ref in ((B, b_in), (S, s_in), (FX, fx_in), (FY, fy_in), (FZ, fz_in)):
        c = pltpu.make_async_copy(ref, C.at[f, 0, pl.ds(2, 16), pl.ds(8, 32)], in_sem.at[f])
        c.start()
        loads.append(c)

    far = [(a, b, c) for a in range(GX) for b in (-1, 0, 1) for c in (-1, 0, 1) if (a, b, c) != (0, 0, 0)]
    far = sorted(far, key=lambda d: -(min(d[0], GX - d[0]) + abs(d[1]) + abs(d[2])))
    bar = pltpu.get_barrier_semaphore()
    for d in far:
        pl.semaphore_signal(bar, inc=1, device_id=dev(d), device_id_type=MESH)

    def start(msgs, ss, rs):
        copies = []
        for k, (d, src, dst) in enumerate(msgs):
            c = pltpu.make_async_remote_copy(
                src_ref=src, dst_ref=dst, send_sem=ss.at[k], recv_sem=rs.at[k],
                device_id=dev(d), device_id_type=MESH)
            c.start()
            copies.append(c)
        return copies

    def finish(copies):
        for c in copies:
            c.wait_recv()
        for c in copies:
            c.wait_send()

    lane128 = iota((1, 128), 1)
    first = [m == 0 for m in me]
    last = [m == s - 1 for m, s in zip(me, sizes)]

    for c in loads:
        c.wait()

    C[FX, 0, 17, 8:40, :] = jnp.where(last[0], 0.0, C[FX, 0, 17, 8:40, :])
    row8 = iota((8, 128), 0)
    lane32 = iota((32, 128), 1)

    def close(x, _):
        C[FY, 0, x, 32:40, :] = jnp.where(last[1] & (row8 == 7), 0.0, C[FY, 0, x, 32:40, :])
        C[FZ, 0, x, 8:40, :] = jnp.where(last[2] & (lane32 == 127), 0.0, C[FZ, 0, x, 8:40, :])
        return 0

    lax.fori_loop(2, 18, close, 0)

    TILES = ((0, 6), (6, 5), (11, 5))

    for t, (x0, n) in enumerate(TILES):
        def pack(i, acc, x0=x0):
            for f in range(5):
                g = i * 5 + f
                v = pltpu.roll(C[f, 0, 2 + x0 + i, 8:40, :], 4 * g + 2, 1)
                acc = jnp.where((lane32 >> 2) == g, v, acc)
            return acc
        ZC[t] = lax.fori_loop(0, n, pack, jnp.zeros((32, 128), F32))

    pl.semaphore_wait(bar, len(far))

    ROWS = {1: (32, 0, 8), -1: (8, 40, 8), 0: (8, 8, 32)}

    def fine_msgs(dirs, xs, field, zsrc, zland, ztiles):
        msgs = []
        for d in dirs:
            dx, dy, dz = d
            sy, ty, ny = ROWS[dy]
            if dz == 0:
                sx, tx, nx = xs[dx]
                msgs.append((d, field(pl.ds(sx, nx), pl.ds(sy, ny)), field(pl.ds(tx, nx), pl.ds(ty, ny))))
            else:
                side = 0 if dz == 1 else 1
                s0, t0, nt = ztiles[dx]
                msgs.append((d, zsrc.at[pl.ds(s0, nt), pl.ds(sy - 8, ny)], zland.at[side, pl.ds(t0, nt), pl.ds(ty, ny)]))
        return msgs

    cfield = lambda xs, ys: C.at[:, 0, xs, ys]
    c_msgs = fine_msgs(ALL26, {1: (17, 1, 1), -1: (2, 18, 1), 0: (2, 2, 16)}, cfield, ZC, LC,
                       {1: (2, 0, 1), 0: (0, 1, 3), -1: (0, 4, 1)})
    for dy in (-1, 0, 1):
        sy, ty, ny = ROWS[dy]
        c_msgs.append(((1, dy, 0), C.at[FX, 0, pl.ds(16, 1), pl.ds(sy, ny)], C.at[FX, 0, pl.ds(0, 1), pl.ds(ty, ny)]))
    c_copies = start(c_msgs, c_s, c_r)

    li, lo = iota((256, 128), 0), iota((256, 128), 1)
    hit = ((li & 127) >> 1) == (lo & 63)
    hit = hit & ((li >> 7) == (lo >> 6))
    odd = (li & 1) == 1
    wa = jnp.where(hit, 1.0 / 16, 0.0)
    wb = jnp.where(li < 128, jnp.where(hit & odd, 1.0 / 16, 0.0), jnp.where(hit, 1.0 / 8, 0.0))

    def mid(i, _):
        x = 2 + 2 * i
        ev, od = pl.ds(8, 16, stride=2), pl.ds(9, 16, stride=2)
        mx = C[FX, 0, x + 1, ev, :] + C[FX, 0, x + 1, od, :]
        my = C[FY, 0, x, od, :] + C[FY, 0, x + 1, od, :]
        mz = (C[FZ, 0, x, ev, :] + C[FZ, 0, x, od, :]) + (C[FZ, 0, x + 1, ev, :] + C[FZ, 0, x + 1, od, :])
        ms = (C[S, 0, x, ev, :] + C[S, 0, x, od, :]) + (C[S, 0, x + 1, ev, :] + C[S, 0, x + 1, od, :])
        RX[0, i, 0:16, :] = mx
        RX[1, i, 0:16, :] = my
        RX[0, i, 16:32, :] = mz
        RX[1, i, 16:32, :] = ms
        return 0

    lax.fori_loop(0, 8, mid, 0)
    for p, w in ((0, wa), (1, wb)):
        lhs = jnp.concatenate(
            [RX[q, :, 16 * p:16 * p + 16, :].reshape(128, 128) for q in (0, 1)], axis=1)
        KP[p, 6:14, 8:24, :] = dot(lhs, w).reshape(8, 16, 128)

    lane16 = iota((16, 128), 1)

    def pack_mid(load, base):
        acc = jnp.zeros((16, 128), F32)
        for x in range(8):
            v = load(x)
            acc = jnp.where((lane16 >> 3) == 2 * x, shift(v, 16 * x - (base + 56), 1), acc)
            acc = jnp.where((lane16 >> 3) == 2 * x + 1, shift(v, 16 * x + 8 - base, 1), acc)
        return acc

    for f in range(4):
        ZK[f] = pack_mid(lambda x: KP[f // 2, 6 + x, 8:24, :], 64 * (f % 2))

    MROWS = {1: (16, 0, 8), -1: (8, 24, 8), 0: (8, 8, 16)}

    def mid_msgs(xs, field, zsrc, zland):
        msgs = []
        for d in ALL26:
            dx, dy, dz = d
            sy, ty, ny = MROWS[dy]
            if dz == 0:
                sx, tx, nx = xs[dx]
                msgs.append((d, field(pl.ds(sx, nx), pl.ds(sy, ny)), field(pl.ds(tx, nx), pl.ds(ty, ny))))
            else:
                side = 0 if dz == 1 else 1
                msgs.append((d, zsrc(pl.ds(sy - 8, ny)), zland(side, 1 - dx, pl.ds(ty, ny))))
        return msgs

    finish(c_copies)

    k_copies = start(
        mid_msgs({1: (8, 0, 6), -1: (6, 14, 5), 0: (6, 6, 8)},
                 lambda xs, ys: KP.at[:, xs, ys],
                 lambda ys: ZK.at[:, ys], lambda side, j, ys: LK.at[side, j, :, ys]), k_s, k_r)

    lane48 = iota((48, 128), 1)
    for j, (x0, n, i0) in enumerate(((0, 2, 3), (2, 6, 0), (8, 5, 0), (13, 5, 0), (18, 2, 0))):
        both = jnp.where((lane48 & 3) >= 2, LC[1, j], LC[0, j])
        LC[0, j] = both

        def spread(i, _, j=j, x0=x0, i0=i0):
            both = LC[0, j]
            for f in range(5):
                C[f, 1, x0 + i, :, :] = pltpu.roll(both, 126 + 128 - 4 * ((i + i0) * 5 + f), 1)
            return 0

        lax.fori_loop(0, n, spread, 0)

    def ld(ref, x):
        return jnp.concatenate([ref[0, x], ref[1, x]], axis=1)

    def ldc(f, x):
        return jnp.concatenate([C[f, 0, x], C[f, 1, x]], axis=1)

    def st(ref, x, v):
        ref[0, x] = v[:, :128]
        ref[1, x] = v[:, 128:]

    t_inv, ((ca, cb),) = cheb_factors(2, 0.5, 2.0)

    def diag0(x, _):
        fy, fz = ldc(FY, x), ldc(FZ, x)
        diag = (ldc(S, x) + ldc(FX, x) + ldc(FX, x - 1)) + (fy + shift(fy, 1, 0)) + (fz + shift(fz, 1, 1))
        inv = 1.0 / diag
        st(ID, x, inv)
        st(D, x, t_inv * inv * ldc(B, x))
        return 0

    lax.fori_loop(1, 19, diag0, 0)

    def residual0(ref, x):
        v = ld(ref, x)
        gy_ = ldc(FY, x) * (v - shift(v, -1, 0))
        gz_ = ldc(FZ, x) * (v - shift(v, -1, 1))
        av = ldc(S, x) * v + ldc(FX, x) * (v - ld(ref, x + 1)) + ldc(FX, x - 1) * (v - ld(ref, x - 1))
        av = av + (gy_ - shift(gy_, 1, 0)) + (gz_ - shift(gz_, 1, 1))
        return v, ldc(B, x) - av

    def pre0(x, _):
        d, r = residual0(D, x)
        v = d + (ca * d + cb * ld(ID, x) * r)
        V[0, x, 8:40, :] = v[8:40, :128]
        return 0

    lax.fori_loop(2, 18, pre0, 0)

    def pack_v(i, acc):
        v = pltpu.roll(V[0, 2 + i, 8:40, :], 4 * i + 2, 1)
        return jnp.where((lane32 >> 2) == i, v, acc)

    ZV[0] = lax.fori_loop(0, 16, pack_v, jnp.zeros((32, 128), F32))
    v_copies = start(
        fine_msgs(ALL26, {1: (16, 0, 2), -1: (2, 18, 2), 0: (2, 2, 16)},
                  lambda xs, ys: V.at[0, xs, ys], ZV, LV, {1: (0, 0, 1), 0: (0, 1, 1), -1: (0, 2, 1)}), v_s, v_r)

    wi, wo = iota((128, 128), 0), iota((128, 128), 1)
    in32 = wo < 32

    def packed(rows, w):
        r = dot(rows, w)
        acc = r[0:8]
        for i in range(1, 4):
            acc = acc + shift(r[8 * i:8 * i + 8], 32 * i, 1)
        return acc

    for f, half in ((0, 0), (1, 64), (2, 0), (3, 64)):
        p = f // 2
        rows = []
        for i in range(4):
            x = 6 + 2 * i
            e0, o0 = KP[p, x, pl.ds(8, 8, stride=2), :], KP[p, x, pl.ds(9, 8, stride=2), :]
            e1, o1 = KP[p, x + 1, pl.ds(8, 8, stride=2), :], KP[p, x + 1, pl.ds(9, 8, stride=2), :]
            rows.append((e1 + o1) if f == 0 else (o0 + o1) if f == 1 else (e0 + o0) + (e1 + o1))
        z = wi - half
        sel = (z >= 0) & (z < 64) & ((z >> 1) == wo) & in32
        if f == 2:
            sel = sel & ((z & 1) == 1)
        K2P[f] = packed(jnp.concatenate(rows, 0), jnp.where(sel, 1.0 / (8 if f == 3 else 16), 0.0))
    rim = [C[FY, 0, 2 + x, 7:8, :] for x in range(16)]
    rim = jnp.concatenate(
        [jnp.broadcast_to((rim[4 * i] + rim[4 * i + 1]) + (rim[4 * i + 2] + rim[4 * i + 3]), (8, 128)) for i in range(4)], 0)
    below = packed(rim, jnp.where(((wi >> 2) == wo) & in32, 1.0 / 256, 0.0))
    K2P[4] = jnp.where(row8 == 0, below, shift(K2P[1], 1, 0))

    def far_msgs(src, land):
        return [(d, src, land(gx, 1 - d[2], pl.ds(8 - 8 * d[1], 8))) for d in far]

    k2_copies = start(far_msgs(K2P, lambda g, j, ys: LK2.at[g, j, :, ys]), k2_s, k2_r)
    LK2[gx, 1, :, 8:16, :] = K2P[...]

    finish(v_copies)
    for j, (x0, n, i0) in enumerate(((0, 2, 14), (2, 16, 0), (18, 2, 0))):
        LV[0, j] = jnp.where((lane48 & 3) >= 2, LV[1, j], LV[0, j])

        def spread_v(i, _, j=j, x0=x0, i0=i0):
            V[1, x0 + i, :, :] = pltpu.roll(LV[0, j], 126 + 128 - 4 * (i + i0), 1)
            return 0

        lax.fori_loop(0, n, spread_v, 0)

    r48, l256 = iota((48, 256), 0), iota((48, 256), 1)
    keep0 = ((r48 >= jnp.where(first[1], 8, 7)) & (r48 < jnp.where(last[1], 40, 41))
             & ((l256 < jnp.where(last[2], 128, 129)) | (l256 > jnp.where(first[2], 255, 254))))

    def res0(x, _):
        _, r = residual0(V, x)
        inside = ((x > 1) | jnp.logical_not(first[0])) & ((x < 18) | jnp.logical_not(last[0]))
        st(D, x, jnp.where(keep0 & inside, r, 0.0))
        return 0

    lax.fori_loop(1, 19, res0, 0)

    def rest0(i, _):
        x = 2 + 2 * i
        v = 0.125 * (ld(D, x - 1) + ld(D, x + 2)) + 0.375 * (ld(D, x) + ld(D, x + 1))
        st(RX, i, v)
        for h in (0, 1):
            rows = [RX[h, i, pl.ds(7 + k, 16, stride=2), :] for k in range(4)]
            RX[h, i, 0:16, :] = 0.125 * (rows[0] + rows[3]) + 0.375 * (rows[1] + rows[2])
        return 0

    lax.fori_loop(0, 8, rest0, 0)
    zin = jnp.where(li < 192, li, li - 256)
    wr = restrict_weights(zin, lo - 32, (lo >= 32) & (lo < 96))
    lhs = jnp.concatenate([RX[h, :, 0:16, :].reshape(128, 128) for h in (0, 1)], axis=1)
    B1[6:14, 8:24, :] = dot(lhs, wr).reshape(8, 16, 128)
    ZB[...] = pack_mid(lambda x: B1[6 + x, 8:24, :], 32)
    b_copies = start(
        mid_msgs({1: (9, 1, 5), -1: (6, 14, 5), 0: (6, 6, 8)},
                 lambda xs, ys: B1.at[xs, ys],
                 lambda ys: ZB.at[ys], lambda side, j, ys: LB.at[side, j, ys]), b_s, b_r)

    finish(k_copies)
    lane32r = iota((32, 128), 1)

    def z_halo(lm, lp, own, q):
        low = pltpu.roll(lm, 24 + 128 - 16 * q, 1)
        high = pltpu.roll(lp, 88 + 128 - 16 * q, 1)
        return jnp.where(lane32r < 32, low, jnp.where(lane32r < 96, own, high))

    MID = ((0, 0, 6, 2), (1, 6, 8, 0), (2, 14, 5, 0))
    for j, x0, n, i0 in MID:
        def spread_k(i, _, j=j, x0=x0, i0=i0):
            for f in range(4):
                own = pltpu.roll(KP[f // 2, x0 + i], 32 if f % 2 == 0 else 96, 1)
                K1[f, x0 + i] = z_halo(LK[0, j, f], LK[1, j, f], own, i + i0)
            return 0

        lax.fori_loop(0, n, spread_k, 0)

    def diag1(x, _):
        fy, fz = K1[1, x], K1[2, x]
        diag = (K1[3, x] + K1[0, x] + K1[0, x - 1]) + (fy + shift(fy, 1, 0)) + (fz + shift(fz, 1, 1))
        I1[x] = 1.0 / diag
        return 0

    lax.fori_loop(1, 19, diag1, 0)

    finish(b_copies)
    for j, x0, n, i0 in ((0, 1, 5, 3), (1, 6, 8, 0), (2, 14, 5, 0)):
        def spread_b(i, _, j=j, x0=x0, i0=i0):
            b = z_halo(LB[0, j], LB[1, j], B1[x0 + i], i + i0)
            B1[x0 + i] = b
            D1[x0 + i] = t_inv * I1[x0 + i] * b
            return 0

        lax.fori_loop(0, n, spread_b, 0)

    def residual(K, ref, b, x, xp, xm, low_y=None):
        v = ref[x]
        fy, fz = K[1, x], K[2, x]
        gz_ = fz * (v - shift(v, -1, 1))
        av = K[3, x] * v + K[0, x] * (v - ref[xp]) + K[0, xm] * (v - ref[xm])
        if low_y is None:
            gy_ = fy * (v - shift(v, -1, 0))
            av = av + (gy_ - shift(gy_, 1, 0))
        else:
            av = av + fy * (v - shift(v, -1, 0)) + low_y * (v - shift(v, 1, 0))
        av = av + (gz_ - shift(gz_, 1, 1))
        return v, b[x] - av

    def pre1(x, _):
        d, r = residual(K1, D1, B1, x, x + 1, x - 1)
        X1[x] = d + (ca * d + cb * I1[x] * r)
        return 0

    lax.fori_loop(2, 18, pre1, 0)

    r32 = iota((32, 128), 0)
    keep1 = ((r32 >= jnp.where(first[1], 8, 7)) & (r32 < jnp.where(last[1], 24, 25))
             & (lane32r >= jnp.where(first[2], 32, 31)) & (lane32r < jnp.where(last[2], 96, 97)))

    def res1(x, _):
        _, r = residual(K1, X1, B1, x, x + 1, x - 1)
        inside = ((x > 5) | jnp.logical_not(first[0])) & ((x < 14) | jnp.logical_not(last[0]))
        D1[x] = jnp.where(keep1 & inside, r, 0.0)
        return 0

    lax.fori_loop(5, 15, res1, 0)

    rows = []
    for i in range(4):
        x = 6 + 2 * i
        RX1[i] = 0.125 * (D1[x - 1] + D1[x + 2]) + 0.375 * (D1[x] + D1[x + 1])
        parts = [RX1[i, pl.ds(7 + k, 8, stride=2), :] for k in range(4)]
        rows.append(0.125 * (parts[0] + parts[3]) + 0.375 * (parts[1] + parts[2]))
    B2P[...] = packed(jnp.concatenate(rows, 0), restrict_weights(wi - 32, wo, in32))
    b2_copies = start(far_msgs(B2P, lambda g, j, ys: LB2.at[g, j, ys]), b2_s, b2_r)
    LB2[gx, 1, 8:16, :] = B2P[...]

    NX2 = 4 * GX
    finish(k2_copies)
    lane24 = iota((24, 128), 1)

    def unpack2(lm, lc, lp, i):
        return jnp.where(lane24 < 32, pltpu.roll(lm, 128 - 32 * i, 1),
                         jnp.where(lane24 < 64, pltpu.roll(lc, 160 - 32 * i, 1), pltpu.roll(lp, 192 - 32 * i, 1)))

    def spread_k2(x, _):
        g, i = x >> 2, x & 3
        for f in range(5):
            K2[f, x] = unpack2(LK2[g, 0, f], LK2[g, 1, f], LK2[g, 2, f], i)
        return 0

    lax.fori_loop(0, NX2, spread_k2, 0)

    def up(x):
        return lax.rem(x + 1, NX2)

    def down(x):
        return lax.rem(x + (NX2 - 1), NX2)

    def diag2(x, _):
        fz = K2[2, x]
        diag = (K2[3, x] + K2[0, x] + K2[0, down(x)]) + (K2[1, x] + K2[4, x]) + (fz + shift(fz, 1, 1))
        I2[x] = 1.0 / diag
        return 0

    lax.fori_loop(0, NX2, diag2, 0)

    t2_inv, factors2 = cheb_factors(6, 0.05, 2.0)
    finish(b2_copies)

    def spread_b2(x, _):
        g, i = x >> 2, x & 3
        b = unpack2(LB2[g, 0], LB2[g, 1], LB2[g, 2], i)
        Y2[x] = b
        d = t2_inv * I2[x] * b
        D2[x] = d
        X2[0, x] = d
        return 0

    lax.fori_loop(0, NX2, spread_b2, 0)

    r24 = iota((24, 128), 0)
    keep2 = ((r24 >= jnp.where(first[1], 8, 4)) & (r24 < jnp.where(last[1], 16, 20))
             & (lane24 >= jnp.where(first[2], 32, 24)) & (lane24 < jnp.where(last[2], 64, 72)))
    for n, (fa, fb) in enumerate(factors2):
        src, dst = X2.at[n % 2], X2.at[1 - n % 2]
        final = n == len(factors2) - 1

        def step(x, _, src=src, dst=dst, fa=fa, fb=fb, final=final):
            v, r = residual(K2, src, Y2, x, up(x), down(x), K2[4, x])
            d = fa * D2[x] + fb * I2[x] * r
            if final:
                dst[x] = jnp.where(keep2, v + d, 0.0)
            else:
                D2[x] = d
                dst[x] = v + d
            return 0

        lax.fori_loop(0, NX2, step, 0)
    x2 = X2.at[len(factors2) % 2]

    wp = prolong_weights(wi - 32, wo - 32)
    z1 = dot(x2[...].reshape(NX2 * 24, 128), wp).reshape(NX2, 24, 128)
    Y2[...] = z1

    def pro_y1(x, _):
        c = Y2[x]
        lower, upper = shift(c, 1, 0), shift(c, -1, 0)
        PY1[x, pl.ds(0, 16, stride=2), :] = (0.75 * c + 0.25 * lower)[4:20]
        PY1[x, pl.ds(1, 16, stride=2), :] = (0.75 * c + 0.25 * upper)[4:20]
        return 0

    lax.fori_loop(0, NX2, pro_y1, 0)

    def pro_x1(i, _):
        a = 4 * gx + (i - 3)

        def slab(k):
            return jnp.where((k >= 0) & (k < NX2), PY1[lax.rem(k + NX2, NX2)], 0.0)

        c = 0.75 * slab(a)
        X1[2 * i] = X1[2 * i] + (c + 0.25 * slab(a - 1))
        X1[2 * i + 1] = X1[2 * i + 1] + (c + 0.25 * slab(a + 1))
        return 0

    lax.fori_loop(1, 9, pro_x1, 0)

    def post1(x, _):
        v, r = residual(K1, X1, B1, x, x + 1, x - 1)
        d = t_inv * I1[x] * r
        D1[x] = d
        T1[x] = v + d
        return 0

    lax.fori_loop(3, 17, post1, 0)
    keep1p = ((r32 >= jnp.where(first[1], 8, 4)) & (r32 < jnp.where(last[1], 24, 28))
              & (lane32r >= jnp.where(first[2], 32, 28)) & (lane32r < jnp.where(last[2], 96, 100)))

    def post1b(x, _):
        v, r = residual(K1, T1, B1, x, x + 1, x - 1)
        inside = ((x > 5) | jnp.logical_not(first[0])) & ((x < 14) | jnp.logical_not(last[0]))
        X1[x] = jnp.where(keep1p & inside, v + (ca * D1[x] + cb * I1[x] * r), 0.0)
        return 0

    lax.fori_loop(4, 16, post1b, 0)

    pi, po = iota((128, 256), 0), iota((128, 256), 1)
    wq = prolong_weights(pi - 32, jnp.where(po < 192, po, po - 256))
    for i in range(12):
        z0 = dot(X1[4 + i], wq)
        lower, upper = shift(z0, 1, 0), shift(z0, -1, 0)
        ev, od = 0.75 * z0 + 0.25 * lower, 0.75 * z0 + 0.25 * upper
        for h in (0, 1):
            PY0[h, i, pl.ds(0, 24, stride=2), :] = ev[4:28, 128 * h:128 * h + 128]
            PY0[h, i, pl.ds(1, 24, stride=2), :] = od[4:28, 128 * h:128 * h + 128]

    def pro_x0(i, _):
        c = 0.75 * ld(PY0, i + 1)
        st(V, 2 * i, ld(V, 2 * i) + (c + 0.25 * ld(PY0, i)))
        st(V, 2 * i + 1, ld(V, 2 * i + 1) + (c + 0.25 * ld(PY0, i + 2)))
        return 0

    lax.fori_loop(0, 10, pro_x0, 0)

    def post0(x, _):
        v, r = residual0(V, x)
        d = t_inv * ld(ID, x) * r
        st(D, x, d)
        st(W, x, v + d)
        return 0

    lax.fori_loop(1, 19, post0, 0)

    def post0b(x, _):
        v, r = residual0(W, x)
        o = v + (ca * ld(D, x) + cb * ld(ID, x) * r)
        out[x - 2] = o[8:40, :128]
        return 0

    lax.fori_loop(2, 18, post0b, 0)


def solution(mesh):
    sizes = tuple(mesh.shape[a] for a in ("gx", "gy", "gz"))
    nfar = 9 * sizes[0] - 1
    nx2 = 4 * sizes[0]

    def vm(*shape):
        return pltpu.VMEM(shape, F32)

    dma = lambda n: pltpu.SemaphoreType.DMA((n,))
    scratch = [
        vm(5, 2, 20, 48, 128), vm(2, 20, 48, 128), vm(2, 20, 48, 128), vm(2, 20, 48, 128), vm(2, 20, 48, 128),
        vm(2, 8, 48, 128), vm(3, 32, 128), vm(2, 5, 48, 128), vm(1, 32, 128), vm(2, 3, 48, 128),
        vm(2, 20, 32, 128), vm(4, 20, 32, 128), vm(4, 16, 128), vm(2, 3, 4, 32, 128),
        vm(20, 32, 128), vm(20, 32, 128), vm(20, 32, 128), vm(20, 32, 128), vm(20, 32, 128),
        vm(16, 128), vm(2, 3, 32, 128), vm(4, 32, 128),
        vm(5, 8, 128), vm(sizes[0], 3, 5, 24, 128), vm(8, 128), vm(sizes[0], 3, 24, 128),
        vm(5, nx2, 24, 128), vm(nx2, 24, 128), vm(2, nx2, 24, 128), vm(nx2, 24, 128), vm(nx2, 24, 128),
        vm(nx2, 32, 128), vm(2, 12, 48, 128),
        dma(5), dma(29), dma(29), dma(26), dma(26), dma(26), dma(26), dma(26), dma(26),
        dma(nfar), dma(nfar), dma(nfar), dma(nfar),
    ]

    def local(right_side, face_x, face_y, face_z, absorb):
        return pl.pallas_call(
            functools.partial(kernel, sizes),
            out_shape=jax.ShapeDtypeStruct(right_side.shape, F32),
            in_specs=[pl.BlockSpec(memory_space=pl.ANY)] * 5,
            out_specs=pl.BlockSpec(memory_space=pltpu.VMEM),
            scratch_shapes=scratch,
            compiler_params=pltpu.CompilerParams(
                collective_id=0, has_side_effects=True, vmem_limit_bytes=40 * 1024 * 1024),
            name="vcycle",
        )(right_side, face_x, face_y, face_z, absorb)

    spec = P("gx", "gy", "gz")
    return jax.shard_map(local, mesh=mesh, in_specs=(spec,) * 5, out_specs=spec, check_vma=False)
```

```python
import functools
import math

import jax
import jax.numpy as jnp
from jax import lax
from jax.experimental import pallas as pl
from jax.experimental.pallas import tpu as pltpu
from jax.sharding import PartitionSpec as P

MESH = pl.DeviceIdType.MESH
F32 = jnp.float32
HI = lax.Precision.HIGHEST

B, S, FY, FZ, FX = range(5)

ALL26 = sorted(
    [(a, b, c) for a in (-1, 0, 1) for b in (-1, 0, 1) for c in (-1, 0, 1) if (a, b, c) != (0, 0, 0)],
    key=lambda d: -sum(map(abs, d)),
)


def cheb_factors(steps, lowest, highest):
    centre = 0.5 * (lowest + highest)
    half = 0.5 * (highest - lowest)
    q = centre / half
    rho = 1.0 / q
    out = []
    for _ in range(steps - 1):
        nxt = 1.0 / (2.0 * q - rho)
        out.append((nxt * rho, 2.0 * nxt / half))
        rho = nxt
    return 1.0 / centre, out


EDGES = [(1, 1), (1, -1), (-1, 1), (-1, -1)]


def iota(shape, dim):
    return lax.broadcasted_iota(jnp.int32, shape, dim)


def dot(a, b):
    return jnp.dot(a, b, precision=HI, preferred_element_type=F32)


def shift(v, amount, axis):
    return pltpu.roll(v, amount % v.shape[axis], axis)


def restrict_weights(z, k, ok):
    t = z - 2 * k
    w = jnp.where((t == 0) | (t == 1), 0.375, jnp.where((t == -1) | (t == 2), 0.125, 0.0))
    return jnp.where(ok, w, 0.0)


def prolong_weights(coarse, fine):
    k = fine >> 1
    side = jnp.where((fine & 1) == 0, k - 1, k + 1)
    return jnp.where(coarse == k, 0.75, jnp.where(coarse == side, 0.25, 0.0))


def loop(lo, hi, body, init=0):
    for i in range(lo, hi):
        init = body(i, init)
    return init


def kernel(sizes, b_in, fx_in, fy_in, fz_in, s_in, out,
           C, ID, V, D, W, RX, ZC, LC, ZV, LV,
           KP, K1, ZK, LK, B1, I1, X1, D1, T1, ZB, LB, RX1,
           K2P, LK2, B2P, LB2, K2, I2, X2, D2, Y2, PY1, PY0,
           CY, CYL, CE, CEL, VY, VYL, VE, VEL, count, in_sem, sems):
    GX, GY, GZ = sizes
    gx, gy, gz = (lax.axis_index(a) for a in ("gx", "gy", "gz"))
    me = (gx, gy, gz)

    def dev(d):
        return tuple(lax.rem(m + (q + s), s) for m, q, s in zip(me, d, sizes))

    loads = []
    for f, ref in ((B, b_in), (S, s_in), (FX, fx_in), (FY, fy_in), (FZ, fz_in)):
        c = pltpu.make_async_copy(ref, C.at[f, 0, pl.ds(2, 16), pl.ds(8, 32)], in_sem.at[f])
        c.start()
        loads.append(c)

    far = [(a, b, c) for a in range(GX) for b in (-1, 0, 1) for c in (-1, 0, 1) if (a, b, c) != (0, 0, 0)]
    far = sorted(far, key=lambda d: -(min(d[0], GX - d[0]) + abs(d[1]) + abs(d[2])))
    bar = pltpu.get_barrier_semaphore()
    for d in far:
        pl.semaphore_signal(bar, inc=1, device_id=dev(d), device_id_type=MESH)

    def start(msgs, ss):
        tiles = 0
        for d, src, dst in msgs:
            tiles += math.prod(dst.shape) // 1024
            c = pltpu.make_async_remote_copy(
                src_ref=src, dst_ref=dst, send_sem=sems.at[ss], recv_sem=sems.at[ss + 1],
                device_id=dev(d), device_id_type=MESH)
            c.start()
        return tiles, ss

    def finish(sent):
        tiles, ss = sent
        span = count.at[pl.ds(0, tiles)]
        pltpu.make_async_copy(span, span, sems.at[ss + 1]).wait()
        pltpu.make_async_copy(span, span, sems.at[ss]).wait()

    lane128 = iota((1, 128), 1)
    first = [m == 0 for m in me]
    last = [m == s - 1 for m, s in zip(me, sizes)]

    for c in loads:
        c.wait()

    C[FX, 0, 17, 8:40, :] = jnp.where(last[0], 0.0, C[FX, 0, 17, 8:40, :])
    row8 = iota((8, 128), 0)
    lane32 = iota((32, 128), 1)

    def close(x, _):
        C[FY, 0, x, 32:40, :] = jnp.where(last[1] & (row8 == 7), 0.0, C[FY, 0, x, 32:40, :])
        C[FZ, 0, x, 8:40, :] = jnp.where(last[2] & (lane32 == 127), 0.0, C[FZ, 0, x, 8:40, :])
        return 0

    loop(2, 18, close, 0)

    TILES = ((0, 6), (6, 5), (11, 5))

    for t, (x0, n) in enumerate(TILES):
        def pack(i, acc, x0=x0):
            for f in range(5):
                g = i * 5 + f
                v = pltpu.roll(C[f, 0, 2 + x0 + i, 8:40, :], 4 * g + 2, 1)
                acc = jnp.where((lane32 >> 2) == g, v, acc)
            return acc
        ZC[t] = loop(0, n, pack, jnp.zeros((32, 128), F32))

    pl.semaphore_wait(bar, len(far))

    ROWS = {1: (32, 0, 8), -1: (8, 40, 8), 0: (8, 8, 32)}

    def fine_msgs(xs, stack, ys, yland, zs, zland, es, eland, ztiles):
        msgs = []
        for d in ALL26:
            dx, dy, dz = d
            if dz != 0:
                sy, ty, ny = ROWS[dy]
                side = 0 if dz == 1 else 1
                s0, t0, nt = ztiles[dx]
                msgs.append((d, zs.at[pl.ds(s0, nt), pl.ds(sy - 8, ny)], zland.at[side, pl.ds(t0, nt), pl.ds(ty, ny)]))
            elif dy == 0:
                sx, tx, nx = xs[dx]
                msgs.append((d, stack(pl.ds(sx, nx)), stack(pl.ds(tx, nx))))
            elif dx == 0:
                side = 0 if dy == 1 else 1
                msgs.append((d, ys.at[side], yland.at[side]))
            else:
                e = EDGES.index((dx, dy))
                msgs.append((d, es.at[e], eland.at[e]))
        return msgs

    CUP = [(f, 39, 7) for f in range(5)] + [(FY, 38, 6)]
    CDOWN = [(f, 8, 40) for f in range(5)]
    C2 = C.reshape(5 * 2 * 20 * 48, 128)

    def crows(f, row):
        return pl.ds((2 * f * 20 + 2) * 48 + row, 16, stride=48)

    CY[1, 5] = jnp.zeros((16, 128), F32)
    for side, rows in ((0, CUP), (1, CDOWN)):
        for k, (f, here, _) in enumerate(rows):
            CY[side, k] = C2[crows(f, here), :]

    def cedge(dx, dy):
        x, tx = (17, 1) if dx == 1 else (2, 18)
        y, ty = (39, 7) if dy == 1 else (8, 40)
        rows = [(f, x, y, tx, ty) for f in range(5)]
        if dy == 1:
            rows.append((FY, x, y - 1, tx, ty - 1))
        if dx == 1:
            rows.append((FX, x - 1, y, tx - 1, ty))
        return rows

    for e, (dx, dy) in enumerate(EDGES):
        for k, (f, x, y, _, _) in enumerate(cedge(dx, dy)):
            CE[e, k:k + 1, :] = C[f, 0, x, y:y + 1, :]

    c_msgs = fine_msgs({1: (17, 1, 1), -1: (2, 18, 1)}, lambda xs: C.at[:, 0, xs, pl.ds(8, 32)],
                       CY, CYL, ZC, LC, CE, CEL, {1: (2, 0, 1), 0: (0, 1, 3), -1: (0, 4, 1)})
    c_msgs.append(((1, 0, 0), C.at[FX, 0, pl.ds(16, 1), pl.ds(8, 32)], C.at[FX, 0, pl.ds(0, 1), pl.ds(8, 32)]))
    c_sent = start(c_msgs, 0)

    li, lo = iota((256, 128), 0), iota((256, 128), 1)
    hit = ((li & 127) >> 1) == (lo & 63)
    hit = hit & ((li >> 7) == (lo >> 6))
    odd = (li & 1) == 1
    wa = jnp.where(hit, 1.0 / 16, 0.0)
    wb = jnp.where(li < 128, jnp.where(hit & odd, 1.0 / 16, 0.0), jnp.where(hit, 1.0 / 8, 0.0))

    def mid(i, _):
        x = 2 + 2 * i
        ev, od = pl.ds(8, 16, stride=2), pl.ds(9, 16, stride=2)
        mx = C[FX, 0, x + 1, ev, :] + C[FX, 0, x + 1, od, :]
        my = C[FY, 0, x, od, :] + C[FY, 0, x + 1, od, :]
        mz = (C[FZ, 0, x, ev, :] + C[FZ, 0, x, od, :]) + (C[FZ, 0, x + 1, ev, :] + C[FZ, 0, x + 1, od, :])
        ms = (C[S, 0, x, ev, :] + C[S, 0, x, od, :]) + (C[S, 0, x + 1, ev, :] + C[S, 0, x + 1, od, :])
        RX[0, i, 0:16, :] = mx
        RX[1, i, 0:16, :] = my
        RX[0, i, 16:32, :] = mz
        RX[1, i, 16:32, :] = ms
        return 0

    loop(0, 8, mid, 0)
    for p, w in ((0, wa), (1, wb)):
        lhs = jnp.concatenate(
            [RX[q, :, 16 * p:16 * p + 16, :].reshape(128, 128) for q in (0, 1)], axis=1)
        KP[p, 6:14, 8:24, :] = dot(lhs, w).reshape(8, 16, 128)

    lane16 = iota((16, 128), 1)

    def pack_mid(load, base):
        acc = jnp.zeros((16, 128), F32)
        for x in range(8):
            v = load(x)
            acc = jnp.where((lane16 >> 3) == 2 * x, shift(v, 16 * x - (base + 56), 1), acc)
            acc = jnp.where((lane16 >> 3) == 2 * x + 1, shift(v, 16 * x + 8 - base, 1), acc)
        return acc

    for f in range(4):
        ZK[f] = pack_mid(lambda x: KP[f // 2, 6 + x, 8:24, :], 64 * (f % 2))

    MROWS = {1: (16, 0, 8), -1: (8, 24, 8), 0: (8, 8, 16)}

    def mid_msgs(xs, field, zsrc, zland):
        msgs = []
        for d in ALL26:
            dx, dy, dz = d
            sy, ty, ny = MROWS[dy]
            if dz == 0:
                sx, tx, nx = xs[dx]
                msgs.append((d, field(pl.ds(sx, nx), pl.ds(sy, ny)), field(pl.ds(tx, nx), pl.ds(ty, ny))))
            else:
                side = 0 if dz == 1 else 1
                msgs.append((d, zsrc(pl.ds(sy - 8, ny)), zland(side, 1 - dx, pl.ds(ty, ny))))
        return msgs

    finish(c_sent)
    for side, rows in ((0, CUP), (1, CDOWN)):
        for k, (f, _, there) in enumerate(rows):
            C2[crows(f, there), :] = CYL[side, k]
    for e, (dx, dy) in enumerate(EDGES):
        for k, (f, _, _, x, y) in enumerate(cedge(dx, dy)):
            C[f, 0, x, y:y + 1, :] = CEL[e, k:k + 1, :]

    lane48 = iota((48, 128), 1)
    for j, (x0, n, i0) in enumerate(((0, 2, 3), (2, 6, 0), (8, 5, 0), (13, 5, 0), (18, 2, 0))):
        both = jnp.where((lane48 & 3) >= 2, LC[1, j], LC[0, j])
        LC[0, j] = both

        def spread(i, _, j=j, x0=x0, i0=i0):
            both = LC[0, j]
            for f in range(5):
                C[f, 1, x0 + i, :, :] = pltpu.roll(both, 126 + 128 - 4 * ((i + i0) * 5 + f), 1)
            return 0

        loop(0, n, spread, 0)

    def ld(ref, x):
        return jnp.concatenate([ref[0, x], ref[1, x]], axis=1)

    def ldc(f, x):
        return jnp.concatenate([C[f, 0, x], C[f, 1, x]], axis=1)

    def st(ref, x, v):
        ref[0, x] = v[:, :128]
        ref[1, x] = v[:, 128:]

    t_inv, ((ca, cb),) = cheb_factors(2, 0.5, 2.0)

    def diag0(x, _):
        fy, fz = ldc(FY, x), ldc(FZ, x)
        diag = (ldc(S, x) + ldc(FX, x) + ldc(FX, x - 1)) + (fy + shift(fy, 1, 0)) + (fz + shift(fz, 1, 1))
        inv = 1.0 / diag
        st(ID, x, inv)
        st(D, x, t_inv * inv * ldc(B, x))
        return 0

    loop(1, 19, diag0, 0)

    def residual0(ref, x):
        v = ld(ref, x)
        gy_ = ldc(FY, x) * (v - shift(v, -1, 0))
        gz_ = ldc(FZ, x) * (v - shift(v, -1, 1))
        av = ldc(S, x) * v + ldc(FX, x) * (v - ld(ref, x + 1)) + ldc(FX, x - 1) * (v - ld(ref, x - 1))
        av = av + (gy_ - shift(gy_, 1, 0)) + (gz_ - shift(gz_, 1, 1))
        return v, ldc(B, x) - av

    def pre0(x, _):
        d, r = residual0(D, x)
        v = d + (ca * d + cb * ld(ID, x) * r)
        V[0, x, 8:40, :] = v[8:40, :128]
        return 0

    loop(2, 18, pre0, 0)

    def pack_v(i, acc):
        v = pltpu.roll(V[0, 2 + i, 8:40, :], 4 * i + 2, 1)
        return jnp.where((lane32 >> 2) == i, v, acc)

    ZV[0] = loop(0, 16, pack_v, jnp.zeros((32, 128), F32))
    V2 = V.reshape(2 * 20 * 48, 128)

    def vrows(row):
        return pl.ds(2 * 48 + row, 16, stride=48)

    for k in (0, 1):
        VY[0, k] = V2[vrows(38 + k), :]
        VY[1, k] = V2[vrows(8 + k), :]

    def vedge(dx, dy):
        x, tx = (16, 0) if dx == 1 else (2, 18)
        y, ty = (38, 6) if dy == 1 else (8, 40)
        return [(x + a, y + b, tx + a, ty + b) for a in (0, 1) for b in (0, 1)]

    for e, (dx, dy) in enumerate(EDGES):
        for k, (x, y, _, _) in enumerate(vedge(dx, dy)):
            VE[e, k:k + 1, :] = V[0, x, y:y + 1, :]
    v_sent = start(fine_msgs({1: (16, 0, 2), -1: (2, 18, 2)}, lambda xs: V.at[0, xs, pl.ds(8, 32)],
                             VY, VYL, ZV, LV, VE, VEL, {1: (0, 0, 1), 0: (0, 1, 1), -1: (0, 2, 1)}), 2)
    k_sent = start(
        mid_msgs({1: (8, 0, 6), -1: (6, 14, 5), 0: (6, 6, 8)},
                 lambda xs, ys: KP.at[:, xs, ys],
                 lambda ys: ZK.at[:, ys], lambda side, j, ys: LK.at[side, j, :, ys]), 4)

    wi, wo = iota((128, 128), 0), iota((128, 128), 1)
    in32 = wo < 32

    def packed(rows, w):
        r = dot(rows, w)
        acc = r[0:8]
        for i in range(1, 4):
            acc = acc + shift(r[8 * i:8 * i + 8], 32 * i, 1)
        return acc

    for f, half in ((0, 0), (1, 64), (2, 0), (3, 64)):
        p = f // 2
        rows = []
        for i in range(4):
            x = 6 + 2 * i
            e0, o0 = KP[p, x, pl.ds(8, 8, stride=2), :], KP[p, x, pl.ds(9, 8, stride=2), :]
            e1, o1 = KP[p, x + 1, pl.ds(8, 8, stride=2), :], KP[p, x + 1, pl.ds(9, 8, stride=2), :]
            rows.append((e1 + o1) if f == 0 else (o0 + o1) if f == 1 else (e0 + o0) + (e1 + o1))
        z = wi - half
        sel = (z >= 0) & (z < 64) & ((z >> 1) == wo) & in32
        if f == 2:
            sel = sel & ((z & 1) == 1)
        K2P[f] = packed(jnp.concatenate(rows, 0), jnp.where(sel, 1.0 / (8 if f == 3 else 16), 0.0))
    rim = [C[FY, 0, 2 + x, 7:8, :] for x in range(16)]
    rim = jnp.concatenate(
        [jnp.broadcast_to((rim[4 * i] + rim[4 * i + 1]) + (rim[4 * i + 2] + rim[4 * i + 3]), (8, 128)) for i in range(4)], 0)
    below = packed(rim, jnp.where(((wi >> 2) == wo) & in32, 1.0 / 256, 0.0))
    K2P[4] = jnp.where(row8 == 0, below, shift(K2P[1], 1, 0))

    def far_msgs(src, land):
        return [(d, src, land(gx, 1 - d[2], pl.ds(8 - 8 * d[1], 8))) for d in far]

    LK2[gx, 1, :, 8:16, :] = K2P[...]

    finish(v_sent)
    for k in (0, 1):
        V2[vrows(6 + k), :] = VYL[0, k]
        V2[vrows(40 + k), :] = VYL[1, k]
    for e, (dx, dy) in enumerate(EDGES):
        for k, (_, _, x, y) in enumerate(vedge(dx, dy)):
            V[0, x, y:y + 1, :] = VEL[e, k:k + 1, :]
    for j, (x0, n, i0) in enumerate(((0, 2, 14), (2, 16, 0), (18, 2, 0))):
        LV[0, j] = jnp.where((lane48 & 3) >= 2, LV[1, j], LV[0, j])

        def spread_v(i, _, j=j, x0=x0, i0=i0):
            V[1, x0 + i, :, :] = pltpu.roll(LV[0, j], 126 + 128 - 4 * (i + i0), 1)
            return 0

        loop(0, n, spread_v, 0)

    r48, l256 = iota((48, 256), 0), iota((48, 256), 1)
    keep0 = ((r48 >= jnp.where(first[1], 8, 7)) & (r48 < jnp.where(last[1], 40, 41))
             & ((l256 < jnp.where(last[2], 128, 129)) | (l256 > jnp.where(first[2], 255, 254))))

    def res0(x, _):
        _, r = residual0(V, x)
        inside = ((x > 1) | jnp.logical_not(first[0])) & ((x < 18) | jnp.logical_not(last[0]))
        st(D, x, jnp.where(keep0 & inside, r, 0.0))
        return 0

    loop(1, 19, res0, 0)

    def rest0(i, _):
        x = 2 + 2 * i
        v = 0.125 * (ld(D, x - 1) + ld(D, x + 2)) + 0.375 * (ld(D, x) + ld(D, x + 1))
        st(RX, i, v)
        for h in (0, 1):
            rows = [RX[h, i, pl.ds(7 + k, 16, stride=2), :] for k in range(4)]
            RX[h, i, 0:16, :] = 0.125 * (rows[0] + rows[3]) + 0.375 * (rows[1] + rows[2])
        return 0

    loop(0, 8, rest0, 0)
    zin = jnp.where(li < 192, li, li - 256)
    wr = restrict_weights(zin, lo - 32, (lo >= 32) & (lo < 96))
    lhs = jnp.concatenate([RX[h, :, 0:16, :].reshape(128, 128) for h in (0, 1)], axis=1)
    B1[6:14, 8:24, :] = dot(lhs, wr).reshape(8, 16, 128)
    ZB[...] = pack_mid(lambda x: B1[6 + x, 8:24, :], 32)
    b_sent = start(
        mid_msgs({1: (9, 1, 5), -1: (6, 14, 5), 0: (6, 6, 8)},
                 lambda xs, ys: B1.at[xs, ys],
                 lambda ys: ZB.at[ys], lambda side, j, ys: LB.at[side, j, ys]), 6)

    k2_sent = start(far_msgs(K2P, lambda g, j, ys: LK2.at[g, j, :, ys]), 8)

    finish(k_sent)
    lane32r = iota((32, 128), 1)

    def z_halo(lm, lp, own, q):
        low = pltpu.roll(lm, 24 + 128 - 16 * q, 1)
        high = pltpu.roll(lp, 88 + 128 - 16 * q, 1)
        return jnp.where(lane32r < 32, low, jnp.where(lane32r < 96, own, high))

    MID = ((0, 0, 6, 2), (1, 6, 8, 0), (2, 14, 5, 0))
    for j, x0, n, i0 in MID:
        def spread_k(i, _, j=j, x0=x0, i0=i0):
            for f in range(4):
                own = pltpu.roll(KP[f // 2, x0 + i], 32 if f % 2 == 0 else 96, 1)
                K1[f, x0 + i] = z_halo(LK[0, j, f], LK[1, j, f], own, i + i0)
            return 0

        loop(0, n, spread_k, 0)

    def diag1(x, _):
        fy, fz = K1[1, x], K1[2, x]
        diag = (K1[3, x] + K1[0, x] + K1[0, x - 1]) + (fy + shift(fy, 1, 0)) + (fz + shift(fz, 1, 1))
        I1[x] = 1.0 / diag
        return 0

    loop(1, 19, diag1, 0)

    finish(b_sent)
    for j, x0, n, i0 in ((0, 1, 5, 3), (1, 6, 8, 0), (2, 14, 5, 0)):
        def spread_b(i, _, j=j, x0=x0, i0=i0):
            b = z_halo(LB[0, j], LB[1, j], B1[x0 + i], i + i0)
            B1[x0 + i] = b
            D1[x0 + i] = t_inv * I1[x0 + i] * b
            return 0

        loop(0, n, spread_b, 0)

    def residual(K, ref, b, x, xp, xm, low_y=None):
        v = ref[x]
        fy, fz = K[1, x], K[2, x]
        gz_ = fz * (v - shift(v, -1, 1))
        av = K[3, x] * v + K[0, x] * (v - ref[xp]) + K[0, xm] * (v - ref[xm])
        if low_y is None:
            gy_ = fy * (v - shift(v, -1, 0))
            av = av + (gy_ - shift(gy_, 1, 0))
        else:
            av = av + fy * (v - shift(v, -1, 0)) + low_y * (v - shift(v, 1, 0))
        av = av + (gz_ - shift(gz_, 1, 1))
        return v, b[x] - av

    def pre1(x, _):
        d, r = residual(K1, D1, B1, x, x + 1, x - 1)
        X1[x] = d + (ca * d + cb * I1[x] * r)
        return 0

    loop(2, 18, pre1, 0)

    r32 = iota((32, 128), 0)
    keep1 = ((r32 >= jnp.where(first[1], 8, 7)) & (r32 < jnp.where(last[1], 24, 25))
             & (lane32r >= jnp.where(first[2], 32, 31)) & (lane32r < jnp.where(last[2], 96, 97)))

    def res1(x, _):
        _, r = residual(K1, X1, B1, x, x + 1, x - 1)
        inside = ((x > 5) | jnp.logical_not(first[0])) & ((x < 14) | jnp.logical_not(last[0]))
        D1[x] = jnp.where(keep1 & inside, r, 0.0)
        return 0

    loop(5, 15, res1, 0)

    rows = []
    for i in range(4):
        x = 6 + 2 * i
        RX1[i] = 0.125 * (D1[x - 1] + D1[x + 2]) + 0.375 * (D1[x] + D1[x + 1])
        parts = [RX1[i, pl.ds(7 + k, 8, stride=2), :] for k in range(4)]
        rows.append(0.125 * (parts[0] + parts[3]) + 0.375 * (parts[1] + parts[2]))
    B2P[...] = packed(jnp.concatenate(rows, 0), restrict_weights(wi - 32, wo, in32))
    b2_sent = start(far_msgs(B2P, lambda g, j, ys: LB2.at[g, j, ys]), 10)
    LB2[gx, 1, 8:16, :] = B2P[...]

    NX2 = 4 * GX
    finish(k2_sent)
    lane24 = iota((24, 128), 1)

    def unpack2(lm, lc, lp, i):
        return jnp.where(lane24 < 32, pltpu.roll(lm, 128 - 32 * i, 1),
                         jnp.where(lane24 < 64, pltpu.roll(lc, 160 - 32 * i, 1), pltpu.roll(lp, 192 - 32 * i, 1)))

    def spread_k2(x, _):
        g, i = x >> 2, x & 3
        for f in range(5):
            K2[f, x] = unpack2(LK2[g, 0, f], LK2[g, 1, f], LK2[g, 2, f], i)
        return 0

    loop(0, NX2, spread_k2, 0)

    def up(x):
        return lax.rem(x + 1, NX2)

    def down(x):
        return lax.rem(x + (NX2 - 1), NX2)

    def diag2(x, _):
        fz = K2[2, x]
        diag = (K2[3, x] + K2[0, x] + K2[0, down(x)]) + (K2[1, x] + K2[4, x]) + (fz + shift(fz, 1, 1))
        I2[x] = 1.0 / diag
        return 0

    loop(0, NX2, diag2, 0)

    t2_inv, factors2 = cheb_factors(6, 0.05, 2.0)
    finish(b2_sent)

    def spread_b2(x, _):
        g, i = x >> 2, x & 3
        b = unpack2(LB2[g, 0], LB2[g, 1], LB2[g, 2], i)
        Y2[x] = b
        d = t2_inv * I2[x] * b
        D2[x] = d
        X2[0, x] = d
        return 0

    loop(0, NX2, spread_b2, 0)

    r24 = iota((24, 128), 0)
    keep2 = ((r24 >= jnp.where(first[1], 8, 4)) & (r24 < jnp.where(last[1], 16, 20))
             & (lane24 >= jnp.where(first[2], 32, 24)) & (lane24 < jnp.where(last[2], 64, 72)))
    for n, (fa, fb) in enumerate(factors2):
        src, dst = X2.at[n % 2], X2.at[1 - n % 2]
        final = n == len(factors2) - 1

        def step(x, _, src=src, dst=dst, fa=fa, fb=fb, final=final):
            v, r = residual(K2, src, Y2, x, up(x), down(x), K2[4, x])
            d = fa * D2[x] + fb * I2[x] * r
            if final:
                dst[x] = jnp.where(keep2, v + d, 0.0)
            else:
                D2[x] = d
                dst[x] = v + d
            return 0

        loop(0, NX2, step, 0)
    x2 = X2.at[len(factors2) % 2]

    wp = prolong_weights(wi - 32, wo - 32)
    z1 = dot(x2[...].reshape(NX2 * 24, 128), wp).reshape(NX2, 24, 128)
    Y2[...] = z1

    def pro_y1(x, _):
        c = Y2[x]
        lower, upper = shift(c, 1, 0), shift(c, -1, 0)
        PY1[x, pl.ds(0, 16, stride=2), :] = (0.75 * c + 0.25 * lower)[4:20]
        PY1[x, pl.ds(1, 16, stride=2), :] = (0.75 * c + 0.25 * upper)[4:20]
        return 0

    loop(0, NX2, pro_y1, 0)

    def pro_x1(i, _):
        a = 4 * gx + (i - 3)

        def slab(k):
            return jnp.where((k >= 0) & (k < NX2), PY1[lax.rem(k + NX2, NX2)], 0.0)

        c = 0.75 * slab(a)
        X1[2 * i] = X1[2 * i] + (c + 0.25 * slab(a - 1))
        X1[2 * i + 1] = X1[2 * i + 1] + (c + 0.25 * slab(a + 1))
        return 0

    loop(1, 9, pro_x1, 0)

    def post1(x, _):
        v, r = residual(K1, X1, B1, x, x + 1, x - 1)
        d = t_inv * I1[x] * r
        D1[x] = d
        T1[x] = v + d
        return 0

    loop(3, 17, post1, 0)
    keep1p = ((r32 >= jnp.where(first[1], 8, 4)) & (r32 < jnp.where(last[1], 24, 28))
              & (lane32r >= jnp.where(first[2], 32, 28)) & (lane32r < jnp.where(last[2], 96, 100)))

    def post1b(x, _):
        v, r = residual(K1, T1, B1, x, x + 1, x - 1)
        inside = ((x > 5) | jnp.logical_not(first[0])) & ((x < 14) | jnp.logical_not(last[0]))
        X1[x] = jnp.where(keep1p & inside, v + (ca * D1[x] + cb * I1[x] * r), 0.0)
        return 0

    loop(4, 16, post1b, 0)

    pi, po = iota((128, 256), 0), iota((128, 256), 1)
    wq = prolong_weights(pi - 32, jnp.where(po < 192, po, po - 256))
    for i in range(12):
        z0 = dot(X1[4 + i], wq)
        lower, upper = shift(z0, 1, 0), shift(z0, -1, 0)
        ev, od = 0.75 * z0 + 0.25 * lower, 0.75 * z0 + 0.25 * upper
        for h in (0, 1):
            PY0[h, i, pl.ds(0, 24, stride=2), :] = ev[4:28, 128 * h:128 * h + 128]
            PY0[h, i, pl.ds(1, 24, stride=2), :] = od[4:28, 128 * h:128 * h + 128]

    def pro_x0(i, _):
        c = 0.75 * ld(PY0, i + 1)
        st(V, 2 * i, ld(V, 2 * i) + (c + 0.25 * ld(PY0, i)))
        st(V, 2 * i + 1, ld(V, 2 * i + 1) + (c + 0.25 * ld(PY0, i + 2)))
        return 0

    loop(0, 10, pro_x0, 0)

    def post0(x, _):
        v, r = residual0(V, x)
        d = t_inv * ld(ID, x) * r
        st(D, x, d)
        st(W, x, v + d)
        return 0

    loop(1, 19, post0, 0)

    def post0b(x, _):
        v, r = residual0(W, x)
        o = v + (ca * ld(D, x) + cb * ld(ID, x) * r)
        out[x - 2] = o[8:40, :128]
        return 0

    loop(2, 18, post0b, 0)


def solution(mesh):
    sizes = tuple(mesh.shape[a] for a in ("gx", "gy", "gz"))
    nx2 = 4 * sizes[0]

    def vm(*shape):
        return pltpu.VMEM(shape, F32)

    dma = lambda n: pltpu.SemaphoreType.DMA((n,))
    scratch = [
        vm(5, 2, 20, 48, 128), vm(2, 20, 48, 128), vm(2, 20, 48, 128), vm(2, 20, 48, 128), vm(2, 20, 48, 128),
        vm(2, 8, 48, 128), vm(3, 32, 128), vm(2, 5, 48, 128), vm(1, 32, 128), vm(2, 3, 48, 128),
        vm(2, 20, 32, 128), vm(4, 20, 32, 128), vm(4, 16, 128), vm(2, 3, 4, 32, 128),
        vm(20, 32, 128), vm(20, 32, 128), vm(20, 32, 128), vm(20, 32, 128), vm(20, 32, 128),
        vm(16, 128), vm(2, 3, 32, 128), vm(4, 32, 128),
        vm(5, 8, 128), vm(sizes[0], 3, 5, 24, 128), vm(8, 128), vm(sizes[0], 3, 24, 128),
        vm(5, nx2, 24, 128), vm(nx2, 24, 128), vm(2, nx2, 24, 128), vm(nx2, 24, 128), vm(nx2, 24, 128),
        vm(nx2, 32, 128), vm(2, 12, 48, 128),
        vm(2, 6, 16, 128), vm(2, 6, 16, 128), vm(4, 8, 128), vm(4, 8, 128),
        vm(2, 2, 16, 128), vm(2, 2, 16, 128), vm(4, 8, 128), vm(4, 8, 128),
        vm(512, 8, 128), dma(5), dma(12),
    ]

    def local(right_side, face_x, face_y, face_z, absorb):
        return pl.pallas_call(
            functools.partial(kernel, sizes),
            out_shape=jax.ShapeDtypeStruct(right_side.shape, F32),
            in_specs=[pl.BlockSpec(memory_space=pltpu.HBM)] * 5,
            out_specs=pl.BlockSpec(memory_space=pltpu.VMEM),
            scratch_shapes=scratch,
            compiler_params=pltpu.CompilerParams(
                collective_id=0, has_side_effects=True, vmem_limit_bytes=62 * 1024 * 1024),
            name="vcycle",
        )(right_side, face_x, face_y, face_z, absorb)

    spec = P("gx", "gy", "gz")
    return jax.shard_map(local, mesh=mesh, in_specs=(spec,) * 5, out_specs=spec, check_vma=False)
```

```python
import functools
import math

import jax
import jax.numpy as jnp
from jax import lax
from jax.experimental import pallas as pl
from jax.experimental.pallas import tpu as pltpu
from jax.sharding import PartitionSpec as P

MESH = pl.DeviceIdType.MESH
F32 = jnp.float32
HI = lax.Precision.HIGHEST

B, S, FY, FZ, FX = range(5)

ALL26 = sorted(
    [(a, b, c) for a in (-1, 0, 1) for b in (-1, 0, 1) for c in (-1, 0, 1) if (a, b, c) != (0, 0, 0)],
    key=lambda d: -sum(map(abs, d)),
)


def cheb_factors(steps, lowest, highest):
    centre = 0.5 * (lowest + highest)
    half = 0.5 * (highest - lowest)
    q = centre / half
    rho = 1.0 / q
    out = []
    for _ in range(steps - 1):
        nxt = 1.0 / (2.0 * q - rho)
        out.append((nxt * rho, 2.0 * nxt / half))
        rho = nxt
    return 1.0 / centre, out


EDGES = [(1, 1), (1, -1), (-1, 1), (-1, -1)]


def iota(shape, dim):
    return lax.broadcasted_iota(jnp.int32, shape, dim)


def dot(a, b):
    return jnp.dot(a, b, precision=HI, preferred_element_type=F32)


def shift(v, amount, axis):
    return pltpu.roll(v, amount % v.shape[axis], axis)


def restrict_weights(z, k, ok):
    t = z - 2 * k
    w = jnp.where((t == 0) | (t == 1), 0.375, jnp.where((t == -1) | (t == 2), 0.125, 0.0))
    return jnp.where(ok, w, 0.0)


def prolong_weights(coarse, fine):
    k = fine >> 1
    side = jnp.where((fine & 1) == 0, k - 1, k + 1)
    return jnp.where(coarse == k, 0.75, jnp.where(coarse == side, 0.25, 0.0))


def loop(lo, hi, body, init=0):
    for i in range(lo, hi):
        init = body(i, init)
    return init


def kernel(sizes, b_in, fx_in, fy_in, fz_in, s_in, out,
           C, ID, V, D, W, RX, ZC, LC, ZV, LV,
           KP, K1, ZK, LK, B1, I1, X1, D1, T1, ZB, LB, RX1,
           K2P, LK2, B2P, LB2, K2, I2, X2, D2, Y2, PY1, PY0,
           CY, CYL, CE, CEL, VY, VYL, VE, VEL, count, in_sem, sems):
    GX, GY, GZ = sizes
    gx, gy, gz = (lax.axis_index(a) for a in ("gx", "gy", "gz"))
    me = (gx, gy, gz)

    def dev(d):
        return tuple(lax.rem(m + (q + s), s) for m, q, s in zip(me, d, sizes))

    loads = []
    for f, ref in ((B, b_in), (S, s_in), (FX, fx_in), (FY, fy_in), (FZ, fz_in)):
        c = pltpu.make_async_copy(ref, C.at[f, 0, pl.ds(2, 16), pl.ds(8, 32)], in_sem.at[f])
        c.start()
        loads.append(c)

    far = [(a, b, c) for a in range(GX) for b in (-1, 0, 1) for c in (-1, 0, 1) if (a, b, c) != (0, 0, 0)]
    far = sorted(far, key=lambda d: -(min(d[0], GX - d[0]) + abs(d[1]) + abs(d[2])))
    bar = pltpu.get_barrier_semaphore()
    for d in far:
        pl.semaphore_signal(bar, inc=1, device_id=dev(d), device_id_type=MESH)

    def start(msgs, ss):
        tiles = 0
        for d, src, dst in msgs:
            tiles += math.prod(dst.shape) // 1024
            c = pltpu.make_async_remote_copy(
                src_ref=src, dst_ref=dst, send_sem=sems.at[ss], recv_sem=sems.at[ss + 1],
                device_id=dev(d), device_id_type=MESH)
            c.start()
        return tiles, ss

    def finish(sent):
        tiles, ss = sent
        span = count.at[pl.ds(0, tiles)]
        pltpu.make_async_copy(span, span, sems.at[ss + 1]).wait()
        pltpu.make_async_copy(span, span, sems.at[ss]).wait()

    lane128 = iota((1, 128), 1)
    first = [m == 0 for m in me]
    last = [m == s - 1 for m, s in zip(me, sizes)]

    for c in loads:
        c.wait()

    C[FX, 0, 17, 8:40, :] = jnp.where(last[0], 0.0, C[FX, 0, 17, 8:40, :])
    row8 = iota((8, 128), 0)
    lane32 = iota((32, 128), 1)

    def close(x, _):
        C[FY, 0, x, 32:40, :] = jnp.where(last[1] & (row8 == 7), 0.0, C[FY, 0, x, 32:40, :])
        C[FZ, 0, x, 8:40, :] = jnp.where(last[2] & (lane32 == 127), 0.0, C[FZ, 0, x, 8:40, :])
        return 0

    loop(2, 18, close, 0)

    TILES = ((0, 6), (6, 5), (11, 5))

    for t, (x0, n) in enumerate(TILES):
        def pack(i, acc, x0=x0):
            for f in range(5):
                g = i * 5 + f
                v = pltpu.roll(C[f, 0, 2 + x0 + i, 8:40, :], 4 * g + 2, 1)
                acc = jnp.where((lane32 >> 2) == g, v, acc)
            return acc
        ZC[t] = loop(0, n, pack, jnp.zeros((32, 128), F32))

    pl.semaphore_wait(bar, len(far))

    ROWS = {1: (32, 0, 8), -1: (8, 40, 8), 0: (8, 8, 32)}

    def fine_msgs(xs, stack, ys, yland, zs, zland, es, eland, ztiles):
        msgs = []
        for d in ALL26:
            dx, dy, dz = d
            if dz != 0:
                sy, ty, ny = ROWS[dy]
                side = 0 if dz == 1 else 1
                s0, t0, nt = ztiles[dx]
                msgs.append((d, zs.at[pl.ds(s0, nt), pl.ds(sy - 8, ny)], zland.at[side, pl.ds(t0, nt), pl.ds(ty, ny)]))
            elif dy == 0:
                sx, tx, nx = xs[dx]
                msgs.append((d, stack(pl.ds(sx, nx)), stack(pl.ds(tx, nx))))
            elif dx == 0:
                side = 0 if dy == 1 else 1
                msgs.append((d, ys.at[side], yland.at[side]))
            else:
                e = EDGES.index((dx, dy))
                msgs.append((d, es.at[e], eland.at[e]))
        return msgs

    CUP = [(f, 39, 7) for f in range(5)] + [(FY, 38, 6)]
    CDOWN = [(f, 8, 40) for f in range(5)]
    C2 = C.reshape(5 * 2 * 20 * 48, 128)

    def crows(f, row):
        return pl.ds((2 * f * 20 + 2) * 48 + row, 16, stride=48)

    CY[1, 5] = jnp.zeros((16, 128), F32)
    for side, rows in ((0, CUP), (1, CDOWN)):
        for k, (f, here, _) in enumerate(rows):
            CY[side, k] = C2[crows(f, here), :]

    def cedge(dx, dy):
        x, tx = (17, 1) if dx == 1 else (2, 18)
        y, ty = (39, 7) if dy == 1 else (8, 40)
        rows = [(f, x, y, tx, ty) for f in range(5)]
        if dy == 1:
            rows.append((FY, x, y - 1, tx, ty - 1))
        if dx == 1:
            rows.append((FX, x - 1, y, tx - 1, ty))
        return rows

    for e, (dx, dy) in enumerate(EDGES):
        for k, (f, x, y, _, _) in enumerate(cedge(dx, dy)):
            CE[e, k:k + 1, :] = C[f, 0, x, y:y + 1, :]

    c_msgs = fine_msgs({1: (17, 1, 1), -1: (2, 18, 1)}, lambda xs: C.at[:, 0, xs, pl.ds(8, 32)],
                       CY, CYL, ZC, LC, CE, CEL, {1: (2, 0, 1), 0: (0, 1, 3), -1: (0, 4, 1)})
    c_msgs.append(((1, 0, 0), C.at[FX, 0, pl.ds(16, 1), pl.ds(8, 32)], C.at[FX, 0, pl.ds(0, 1), pl.ds(8, 32)]))
    c_sent = start(c_msgs, 0)

    li, lo = iota((256, 128), 0), iota((256, 128), 1)
    hit = ((li & 127) >> 1) == (lo & 63)
    hit = hit & ((li >> 7) == (lo >> 6))
    odd = (li & 1) == 1
    wa = jnp.where(hit, 1.0 / 16, 0.0)
    wb = jnp.where(li < 128, jnp.where(hit & odd, 1.0 / 16, 0.0), jnp.where(hit, 1.0 / 8, 0.0))

    def mid(i, _):
        x = 2 + 2 * i
        ev, od = pl.ds(8, 16, stride=2), pl.ds(9, 16, stride=2)
        mx = C[FX, 0, x + 1, ev, :] + C[FX, 0, x + 1, od, :]
        my = C[FY, 0, x, od, :] + C[FY, 0, x + 1, od, :]
        mz = (C[FZ, 0, x, ev, :] + C[FZ, 0, x, od, :]) + (C[FZ, 0, x + 1, ev, :] + C[FZ, 0, x + 1, od, :])
        ms = (C[S, 0, x, ev, :] + C[S, 0, x, od, :]) + (C[S, 0, x + 1, ev, :] + C[S, 0, x + 1, od, :])
        RX[0, i, 0:16, :] = mx
        RX[1, i, 0:16, :] = my
        RX[0, i, 16:32, :] = mz
        RX[1, i, 16:32, :] = ms
        return 0

    loop(0, 8, mid, 0)
    for p, w in ((0, wa), (1, wb)):
        lhs = jnp.concatenate(
            [RX[q, :, 16 * p:16 * p + 16, :].reshape(128, 128) for q in (0, 1)], axis=1)
        KP[p, 6:14, 8:24, :] = dot(lhs, w).reshape(8, 16, 128)

    lane16 = iota((16, 128), 1)

    def pack_mid(load, base):
        acc = jnp.zeros((16, 128), F32)
        for x in range(8):
            v = load(x)
            acc = jnp.where((lane16 >> 3) == 2 * x, shift(v, 16 * x - (base + 56), 1), acc)
            acc = jnp.where((lane16 >> 3) == 2 * x + 1, shift(v, 16 * x + 8 - base, 1), acc)
        return acc

    for f in range(4):
        ZK[f] = pack_mid(lambda x: KP[f // 2, 6 + x, 8:24, :], 64 * (f % 2))

    MROWS = {1: (16, 0, 8), -1: (8, 24, 8), 0: (8, 8, 16)}

    def mid_msgs(xs, field, zsrc, zland):
        msgs = []
        for d in ALL26:
            dx, dy, dz = d
            sy, ty, ny = MROWS[dy]
            if dz == 0:
                sx, tx, nx = xs[dx]
                msgs.append((d, field(pl.ds(sx, nx), pl.ds(sy, ny)), field(pl.ds(tx, nx), pl.ds(ty, ny))))
            else:
                side = 0 if dz == 1 else 1
                msgs.append((d, zsrc(pl.ds(sy - 8, ny)), zland(side, 1 - dx, pl.ds(ty, ny))))
        return msgs

    finish(c_sent)
    for side, rows in ((0, CUP), (1, CDOWN)):
        for k, (f, _, there) in enumerate(rows):
            C2[crows(f, there), :] = CYL[side, k]
    for e, (dx, dy) in enumerate(EDGES):
        for k, (f, _, _, x, y) in enumerate(cedge(dx, dy)):
            C[f, 0, x, y:y + 1, :] = CEL[e, k:k + 1, :]

    lane48 = iota((48, 128), 1)
    for j, (x0, n, i0) in enumerate(((0, 2, 3), (2, 6, 0), (8, 5, 0), (13, 5, 0), (18, 2, 0))):
        both = jnp.where((lane48 & 3) >= 2, LC[1, j], LC[0, j])
        LC[0, j] = both

        def spread(i, _, j=j, x0=x0, i0=i0):
            both = LC[0, j]
            for f in range(5):
                C[f, 1, x0 + i, :, :] = pltpu.roll(both, 126 + 128 - 4 * ((i + i0) * 5 + f), 1)
            return 0

        loop(0, n, spread, 0)

    def ld(ref, x):
        return jnp.concatenate([ref[0, x], ref[1, x]], axis=1)

    def ldc(f, x):
        return jnp.concatenate([C[f, 0, x], C[f, 1, x]], axis=1)

    def st(ref, x, v):
        ref[0, x] = v[:, :128]
        ref[1, x] = v[:, 128:]

    t_inv, ((ca, cb),) = cheb_factors(2, 0.5, 2.0)

    def diag0(x, _):
        fy, fz = ldc(FY, x), ldc(FZ, x)
        diag = (ldc(S, x) + ldc(FX, x) + ldc(FX, x - 1)) + (fy + shift(fy, 1, 0)) + (fz + shift(fz, 1, 1))
        inv = 1.0 / diag
        st(ID, x, inv)
        st(D, x, t_inv * inv * ldc(B, x))
        return 0

    loop(1, 19, diag0, 0)

    def residual0(ref, x):
        v = ld(ref, x)
        gy_ = ldc(FY, x) * (v - shift(v, -1, 0))
        gz_ = ldc(FZ, x) * (v - shift(v, -1, 1))
        av = ldc(S, x) * v + ldc(FX, x) * (v - ld(ref, x + 1)) + ldc(FX, x - 1) * (v - ld(ref, x - 1))
        av = av + (gy_ - shift(gy_, 1, 0)) + (gz_ - shift(gz_, 1, 1))
        return v, ldc(B, x) - av

    def own_residual0(ref, x):
        wide, fy = ref[0, x], C[FY, 0, x]
        flux = fy * (wide - shift(wide, -1, 0))
        av = (flux - shift(flux, 1, 0))[8:40]
        v, side = wide[8:40], ref[1, x, 8:40, :]
        fz = C[FZ, 0, x, 8:40, :]
        low_z = shift(jnp.where(lane32 == 127, C[FZ, 1, x, 8:40, :], fz), 1, 1)
        av = av + fz * (v - shift(jnp.where(lane32 == 0, side, v), -1, 1))
        av = av + low_z * (v - shift(jnp.where(lane32 == 127, side, v), 1, 1))
        av = av + C[FX, 0, x, 8:40, :] * (v - ref[0, x + 1, 8:40, :])
        av = av + C[FX, 0, x - 1, 8:40, :] * (v - ref[0, x - 1, 8:40, :])
        return v, C[B, 0, x, 8:40, :] - (av + C[S, 0, x, 8:40, :] * v)

    def pre0(x, _):
        d, r = own_residual0(D, x)
        V[0, x, 8:40, :] = d + (ca * d + cb * ID[0, x, 8:40, :] * r)
        return 0

    loop(2, 18, pre0, 0)

    def pack_v(i, acc):
        v = pltpu.roll(V[0, 2 + i, 8:40, :], 4 * i + 2, 1)
        return jnp.where((lane32 >> 2) == i, v, acc)

    ZV[0] = loop(0, 16, pack_v, jnp.zeros((32, 128), F32))
    V2 = V.reshape(2 * 20 * 48, 128)

    def vrows(row):
        return pl.ds(2 * 48 + row, 16, stride=48)

    for k in (0, 1):
        VY[0, k] = V2[vrows(38 + k), :]
        VY[1, k] = V2[vrows(8 + k), :]

    def vedge(dx, dy):
        x, tx = (16, 0) if dx == 1 else (2, 18)
        y, ty = (38, 6) if dy == 1 else (8, 40)
        return [(x + a, y + b, tx + a, ty + b) for a in (0, 1) for b in (0, 1)]

    for e, (dx, dy) in enumerate(EDGES):
        for k, (x, y, _, _) in enumerate(vedge(dx, dy)):
            VE[e, k:k + 1, :] = V[0, x, y:y + 1, :]
    v_sent = start(fine_msgs({1: (16, 0, 2), -1: (2, 18, 2)}, lambda xs: V.at[0, xs, pl.ds(8, 32)],
                             VY, VYL, ZV, LV, VE, VEL, {1: (0, 0, 1), 0: (0, 1, 1), -1: (0, 2, 1)}), 2)
    k_sent = start(
        mid_msgs({1: (8, 0, 6), -1: (6, 14, 5), 0: (6, 6, 8)},
                 lambda xs, ys: KP.at[:, xs, ys],
                 lambda ys: ZK.at[:, ys], lambda side, j, ys: LK.at[side, j, :, ys]), 4)

    wi, wo = iota((128, 128), 0), iota((128, 128), 1)
    in32 = wo < 32

    def packed(rows, w):
        r = dot(rows, w)
        acc = r[0:8]
        for i in range(1, 4):
            acc = acc + shift(r[8 * i:8 * i + 8], 32 * i, 1)
        return acc

    for f, half in ((0, 0), (1, 64), (2, 0), (3, 64)):
        p = f // 2
        rows = []
        for i in range(4):
            x = 6 + 2 * i
            e0, o0 = KP[p, x, pl.ds(8, 8, stride=2), :], KP[p, x, pl.ds(9, 8, stride=2), :]
            e1, o1 = KP[p, x + 1, pl.ds(8, 8, stride=2), :], KP[p, x + 1, pl.ds(9, 8, stride=2), :]
            rows.append((e1 + o1) if f == 0 else (o0 + o1) if f == 1 else (e0 + o0) + (e1 + o1))
        z = wi - half
        sel = (z >= 0) & (z < 64) & ((z >> 1) == wo) & in32
        if f == 2:
            sel = sel & ((z & 1) == 1)
        K2P[f] = packed(jnp.concatenate(rows, 0), jnp.where(sel, 1.0 / (8 if f == 3 else 16), 0.0))
    rim = [C[FY, 0, 2 + x, 7:8, :] for x in range(16)]
    rim = jnp.concatenate(
        [jnp.broadcast_to((rim[4 * i] + rim[4 * i + 1]) + (rim[4 * i + 2] + rim[4 * i + 3]), (8, 128)) for i in range(4)], 0)
    below = packed(rim, jnp.where(((wi >> 2) == wo) & in32, 1.0 / 256, 0.0))
    K2P[4] = jnp.where(row8 == 0, below, shift(K2P[1], 1, 0))

    def far_msgs(src, land):
        return [(d, src, land(gx, 1 - d[2], pl.ds(8 - 8 * d[1], 8))) for d in far]

    LK2[gx, 1, :, 8:16, :] = K2P[...]

    finish(v_sent)
    for k in (0, 1):
        V2[vrows(6 + k), :] = VYL[0, k]
        V2[vrows(40 + k), :] = VYL[1, k]
    for e, (dx, dy) in enumerate(EDGES):
        for k, (_, _, x, y) in enumerate(vedge(dx, dy)):
            V[0, x, y:y + 1, :] = VEL[e, k:k + 1, :]
    for j, (x0, n, i0) in enumerate(((0, 2, 14), (2, 16, 0), (18, 2, 0))):
        LV[0, j] = jnp.where((lane48 & 3) >= 2, LV[1, j], LV[0, j])

        def spread_v(i, _, j=j, x0=x0, i0=i0):
            V[1, x0 + i, :, :] = pltpu.roll(LV[0, j], 126 + 128 - 4 * (i + i0), 1)
            return 0

        loop(0, n, spread_v, 0)

    r48, l256 = iota((48, 256), 0), iota((48, 256), 1)
    keep0 = ((r48 >= jnp.where(first[1], 8, 7)) & (r48 < jnp.where(last[1], 40, 41))
             & ((l256 < jnp.where(last[2], 128, 129)) | (l256 > jnp.where(first[2], 255, 254))))

    def res0(x, _):
        _, r = residual0(V, x)
        inside = ((x > 1) | jnp.logical_not(first[0])) & ((x < 18) | jnp.logical_not(last[0]))
        st(D, x, jnp.where(keep0 & inside, r, 0.0))
        return 0

    loop(1, 19, res0, 0)

    def rest0(i, _):
        x = 2 + 2 * i
        v = 0.125 * (ld(D, x - 1) + ld(D, x + 2)) + 0.375 * (ld(D, x) + ld(D, x + 1))
        st(RX, i, v)
        for h in (0, 1):
            rows = [RX[h, i, pl.ds(7 + k, 16, stride=2), :] for k in range(4)]
            RX[h, i, 0:16, :] = 0.125 * (rows[0] + rows[3]) + 0.375 * (rows[1] + rows[2])
        return 0

    loop(0, 8, rest0, 0)
    zin = jnp.where(li < 192, li, li - 256)
    wr = restrict_weights(zin, lo - 32, (lo >= 32) & (lo < 96))
    lhs = jnp.concatenate([RX[h, :, 0:16, :].reshape(128, 128) for h in (0, 1)], axis=1)
    B1[6:14, 8:24, :] = dot(lhs, wr).reshape(8, 16, 128)
    ZB[...] = pack_mid(lambda x: B1[6 + x, 8:24, :], 32)
    b_sent = start(
        mid_msgs({1: (9, 1, 5), -1: (6, 14, 5), 0: (6, 6, 8)},
                 lambda xs, ys: B1.at[xs, ys],
                 lambda ys: ZB.at[ys], lambda side, j, ys: LB.at[side, j, ys]), 6)

    k2_sent = start(far_msgs(K2P, lambda g, j, ys: LK2.at[g, j, :, ys]), 8)

    finish(k_sent)
    lane32r = iota((32, 128), 1)

    def z_halo(lm, lp, own, q):
        low = pltpu.roll(lm, 24 + 128 - 16 * q, 1)
        high = pltpu.roll(lp, 88 + 128 - 16 * q, 1)
        return jnp.where(lane32r < 32, low, jnp.where(lane32r < 96, own, high))

    MID = ((0, 0, 6, 2), (1, 6, 8, 0), (2, 14, 5, 0))
    for j, x0, n, i0 in MID:
        def spread_k(i, _, j=j, x0=x0, i0=i0):
            for f in range(4):
                own = pltpu.roll(KP[f // 2, x0 + i], 32 if f % 2 == 0 else 96, 1)
                K1[f, x0 + i] = z_halo(LK[0, j, f], LK[1, j, f], own, i + i0)
            return 0

        loop(0, n, spread_k, 0)

    def diag1(x, _):
        fy, fz = K1[1, x], K1[2, x]
        diag = (K1[3, x] + K1[0, x] + K1[0, x - 1]) + (fy + shift(fy, 1, 0)) + (fz + shift(fz, 1, 1))
        I1[x] = 1.0 / diag
        return 0

    loop(1, 19, diag1, 0)

    finish(b_sent)
    for j, x0, n, i0 in ((0, 1, 5, 3), (1, 6, 8, 0), (2, 14, 5, 0)):
        def spread_b(i, _, j=j, x0=x0, i0=i0):
            b = z_halo(LB[0, j], LB[1, j], B1[x0 + i], i + i0)
            B1[x0 + i] = b
            D1[x0 + i] = t_inv * I1[x0 + i] * b
            return 0

        loop(0, n, spread_b, 0)

    def residual(K, ref, b, x, xp, xm, low_y=None):
        v = ref[x]
        fy, fz = K[1, x], K[2, x]
        gz_ = fz * (v - shift(v, -1, 1))
        av = K[3, x] * v + K[0, x] * (v - ref[xp]) + K[0, xm] * (v - ref[xm])
        if low_y is None:
            gy_ = fy * (v - shift(v, -1, 0))
            av = av + (gy_ - shift(gy_, 1, 0))
        else:
            av = av + fy * (v - shift(v, -1, 0)) + low_y * (v - shift(v, 1, 0))
        av = av + (gz_ - shift(gz_, 1, 1))
        return v, b[x] - av

    def pre1(x, _):
        d, r = residual(K1, D1, B1, x, x + 1, x - 1)
        X1[x] = d + (ca * d + cb * I1[x] * r)
        return 0

    loop(2, 18, pre1, 0)

    r32 = iota((32, 128), 0)
    keep1 = ((r32 >= jnp.where(first[1], 8, 7)) & (r32 < jnp.where(last[1], 24, 25))
             & (lane32r >= jnp.where(first[2], 32, 31)) & (lane32r < jnp.where(last[2], 96, 97)))

    def res1(x, _):
        _, r = residual(K1, X1, B1, x, x + 1, x - 1)
        inside = ((x > 5) | jnp.logical_not(first[0])) & ((x < 14) | jnp.logical_not(last[0]))
        D1[x] = jnp.where(keep1 & inside, r, 0.0)
        return 0

    loop(5, 15, res1, 0)

    rows = []
    for i in range(4):
        x = 6 + 2 * i
        RX1[i] = 0.125 * (D1[x - 1] + D1[x + 2]) + 0.375 * (D1[x] + D1[x + 1])
        parts = [RX1[i, pl.ds(7 + k, 8, stride=2), :] for k in range(4)]
        rows.append(0.125 * (parts[0] + parts[3]) + 0.375 * (parts[1] + parts[2]))
    B2P[...] = packed(jnp.concatenate(rows, 0), restrict_weights(wi - 32, wo, in32))
    b2_sent = start(far_msgs(B2P, lambda g, j, ys: LB2.at[g, j, ys]), 10)
    LB2[gx, 1, 8:16, :] = B2P[...]

    NX2 = 4 * GX
    finish(k2_sent)
    lane24 = iota((24, 128), 1)

    def unpack2(lm, lc, lp, i):
        return jnp.where(lane24 < 32, pltpu.roll(lm, 128 - 32 * i, 1),
                         jnp.where(lane24 < 64, pltpu.roll(lc, 160 - 32 * i, 1), pltpu.roll(lp, 192 - 32 * i, 1)))

    def spread_k2(x, _):
        g, i = x >> 2, x & 3
        for f in range(5):
            K2[f, x] = unpack2(LK2[g, 0, f], LK2[g, 1, f], LK2[g, 2, f], i)
        return 0

    loop(0, NX2, spread_k2, 0)

    def up(x):
        return lax.rem(x + 1, NX2)

    def down(x):
        return lax.rem(x + (NX2 - 1), NX2)

    def diag2(x, _):
        fz = K2[2, x]
        diag = (K2[3, x] + K2[0, x] + K2[0, down(x)]) + (K2[1, x] + K2[4, x]) + (fz + shift(fz, 1, 1))
        I2[x] = 1.0 / diag
        return 0

    loop(0, NX2, diag2, 0)

    t2_inv, factors2 = cheb_factors(6, 0.05, 2.0)
    finish(b2_sent)

    def spread_b2(x, _):
        g, i = x >> 2, x & 3
        b = unpack2(LB2[g, 0], LB2[g, 1], LB2[g, 2], i)
        Y2[x] = b
        d = t2_inv * I2[x] * b
        D2[x] = d
        X2[0, x] = d
        return 0

    loop(0, NX2, spread_b2, 0)

    r24 = iota((24, 128), 0)
    keep2 = ((r24 >= jnp.where(first[1], 8, 4)) & (r24 < jnp.where(last[1], 16, 20))
             & (lane24 >= jnp.where(first[2], 32, 24)) & (lane24 < jnp.where(last[2], 64, 72)))
    for n, (fa, fb) in enumerate(factors2):
        src, dst = X2.at[n % 2], X2.at[1 - n % 2]
        final = n == len(factors2) - 1

        def step(x, _, src=src, dst=dst, fa=fa, fb=fb, final=final):
            v, r = residual(K2, src, Y2, x, up(x), down(x), K2[4, x])
            d = fa * D2[x] + fb * I2[x] * r
            if final:
                dst[x] = jnp.where(keep2, v + d, 0.0)
            else:
                D2[x] = d
                dst[x] = v + d
            return 0

        loop(0, NX2, step, 0)
    x2 = X2.at[len(factors2) % 2]

    wp = prolong_weights(wi - 32, wo - 32)
    z1 = dot(x2[...].reshape(NX2 * 24, 128), wp).reshape(NX2, 24, 128)
    Y2[...] = z1

    def pro_y1(x, _):
        c = Y2[x]
        lower, upper = shift(c, 1, 0), shift(c, -1, 0)
        PY1[x, pl.ds(0, 16, stride=2), :] = (0.75 * c + 0.25 * lower)[4:20]
        PY1[x, pl.ds(1, 16, stride=2), :] = (0.75 * c + 0.25 * upper)[4:20]
        return 0

    loop(0, NX2, pro_y1, 0)

    def pro_x1(i, _):
        a = 4 * gx + (i - 3)

        def slab(k):
            return jnp.where((k >= 0) & (k < NX2), PY1[lax.rem(k + NX2, NX2)], 0.0)

        c = 0.75 * slab(a)
        X1[2 * i] = X1[2 * i] + (c + 0.25 * slab(a - 1))
        X1[2 * i + 1] = X1[2 * i + 1] + (c + 0.25 * slab(a + 1))
        return 0

    loop(1, 9, pro_x1, 0)

    def post1(x, _):
        v, r = residual(K1, X1, B1, x, x + 1, x - 1)
        d = t_inv * I1[x] * r
        D1[x] = d
        T1[x] = v + d
        return 0

    loop(3, 17, post1, 0)
    keep1p = ((r32 >= jnp.where(first[1], 8, 4)) & (r32 < jnp.where(last[1], 24, 28))
              & (lane32r >= jnp.where(first[2], 32, 28)) & (lane32r < jnp.where(last[2], 96, 100)))

    def post1b(x, _):
        v, r = residual(K1, T1, B1, x, x + 1, x - 1)
        inside = ((x > 5) | jnp.logical_not(first[0])) & ((x < 14) | jnp.logical_not(last[0]))
        X1[x] = jnp.where(keep1p & inside, v + (ca * D1[x] + cb * I1[x] * r), 0.0)
        return 0

    loop(4, 16, post1b, 0)

    pi, po = iota((128, 256), 0), iota((128, 256), 1)
    wq = prolong_weights(pi - 32, jnp.where(po < 192, po, po - 256))
    for i in range(12):
        z0 = dot(X1[4 + i], wq)
        lower, upper = shift(z0, 1, 0), shift(z0, -1, 0)
        ev, od = 0.75 * z0 + 0.25 * lower, 0.75 * z0 + 0.25 * upper
        for h in (0, 1):
            PY0[h, i, pl.ds(0, 24, stride=2), :] = ev[4:28, 128 * h:128 * h + 128]
            PY0[h, i, pl.ds(1, 24, stride=2), :] = od[4:28, 128 * h:128 * h + 128]

    def pro_x0(i, _):
        c = 0.75 * ld(PY0, i + 1)
        st(V, 2 * i, ld(V, 2 * i) + (c + 0.25 * ld(PY0, i)))
        st(V, 2 * i + 1, ld(V, 2 * i + 1) + (c + 0.25 * ld(PY0, i + 2)))
        return 0

    loop(0, 10, pro_x0, 0)

    def post0(x, _):
        v, r = residual0(V, x)
        d = t_inv * ld(ID, x) * r
        st(D, x, d)
        st(W, x, v + d)
        return 0

    loop(1, 19, post0, 0)

    def post0b(x, _):
        v, r = own_residual0(W, x)
        out[x - 2] = v + (ca * D[0, x, 8:40, :] + cb * ID[0, x, 8:40, :] * r)
        return 0

    loop(2, 18, post0b, 0)


def solution(mesh):
    sizes = tuple(mesh.shape[a] for a in ("gx", "gy", "gz"))
    nx2 = 4 * sizes[0]

    def vm(*shape):
        return pltpu.VMEM(shape, F32)

    dma = lambda n: pltpu.SemaphoreType.DMA((n,))
    scratch = [
        vm(5, 2, 20, 48, 128), vm(2, 20, 48, 128), vm(2, 20, 48, 128), vm(2, 20, 48, 128), vm(2, 20, 48, 128),
        vm(2, 8, 48, 128), vm(3, 32, 128), vm(2, 5, 48, 128), vm(1, 32, 128), vm(2, 3, 48, 128),
        vm(2, 20, 32, 128), vm(4, 20, 32, 128), vm(4, 16, 128), vm(2, 3, 4, 32, 128),
        vm(20, 32, 128), vm(20, 32, 128), vm(20, 32, 128), vm(20, 32, 128), vm(20, 32, 128),
        vm(16, 128), vm(2, 3, 32, 128), vm(4, 32, 128),
        vm(5, 8, 128), vm(sizes[0], 3, 5, 24, 128), vm(8, 128), vm(sizes[0], 3, 24, 128),
        vm(5, nx2, 24, 128), vm(nx2, 24, 128), vm(2, nx2, 24, 128), vm(nx2, 24, 128), vm(nx2, 24, 128),
        vm(nx2, 32, 128), vm(2, 12, 48, 128),
        vm(2, 6, 16, 128), vm(2, 6, 16, 128), vm(4, 8, 128), vm(4, 8, 128),
        vm(2, 2, 16, 128), vm(2, 2, 16, 128), vm(4, 8, 128), vm(4, 8, 128),
        vm(512, 8, 128), dma(5), dma(12),
    ]

    def local(right_side, face_x, face_y, face_z, absorb):
        return pl.pallas_call(
            functools.partial(kernel, sizes),
            out_shape=jax.ShapeDtypeStruct(right_side.shape, F32),
            in_specs=[pl.BlockSpec(memory_space=pltpu.HBM)] * 5,
            out_specs=pl.BlockSpec(memory_space=pltpu.VMEM),
            scratch_shapes=scratch,
            compiler_params=pltpu.CompilerParams(
                collective_id=0, has_side_effects=True, vmem_limit_bytes=62 * 1024 * 1024),
            name="vcycle",
        )(right_side, face_x, face_y, face_z, absorb)

    spec = P("gx", "gy", "gz")
    return jax.shard_map(local, mesh=mesh, in_specs=(spec,) * 5, out_specs=spec, check_vma=False)
```

```python
import functools
import math

import jax
import jax.numpy as jnp
from jax import lax
from jax.experimental import pallas as pl
from jax.experimental.pallas import tpu as pltpu
from jax.sharding import PartitionSpec as P

MESH = pl.DeviceIdType.MESH
F32 = jnp.float32
HI = lax.Precision.HIGHEST

B, S, FY, FZ, FX = range(5)

ALL26 = sorted(
    [(a, b, c) for a in (-1, 0, 1) for b in (-1, 0, 1) for c in (-1, 0, 1) if (a, b, c) != (0, 0, 0)],
    key=lambda d: -sum(map(abs, d)),
)


def cheb_factors(steps, lowest, highest):
    centre = 0.5 * (lowest + highest)
    half = 0.5 * (highest - lowest)
    q = centre / half
    rho = 1.0 / q
    out = []
    for _ in range(steps - 1):
        nxt = 1.0 / (2.0 * q - rho)
        out.append((nxt * rho, 2.0 * nxt / half))
        rho = nxt
    return 1.0 / centre, out


EDGES = [(1, 1), (1, -1), (-1, 1), (-1, -1)]


def iota(shape, dim):
    return lax.broadcasted_iota(jnp.int32, shape, dim)


def dot(a, b):
    return jnp.dot(a, b, precision=HI, preferred_element_type=F32)


def shift(v, amount, axis):
    return pltpu.roll(v, amount % v.shape[axis], axis)


def restrict_weights(z, k, ok):
    t = z - 2 * k
    w = jnp.where((t == 0) | (t == 1), 0.375, jnp.where((t == -1) | (t == 2), 0.125, 0.0))
    return jnp.where(ok, w, 0.0)


def prolong_weights(coarse, fine):
    k = fine >> 1
    side = jnp.where((fine & 1) == 0, k - 1, k + 1)
    return jnp.where(coarse == k, 0.75, jnp.where(coarse == side, 0.25, 0.0))


def loop(lo, hi, body, init=0, chunks=1):
    u = (hi - lo) // chunks
    if chunks == 1:
        for i in range(lo, hi):
            init = body(i, init)
        return init

    def chunk(c, carry):
        for k in range(u):
            carry = body(lo + c * u + k, carry)
        return carry

    return lax.fori_loop(0, chunks, chunk, init)


def kernel(sizes, b_in, fx_in, fy_in, fz_in, s_in, out,
           C, ID, V, D, W, RX, ZC, LC, ZV, LV,
           KP, K1, ZK, LK, B1, I1, X1, D1, T1, ZB, LB, RX1,
           K2P, LK2, B2P, LB2, K2, I2, X2, D2, Y2, PY1, PY0,
           CY, CYL, CE, CEL, VY, VYL, VE, VEL, count, in_sem, sems):
    GX, GY, GZ = sizes
    gx, gy, gz = (lax.axis_index(a) for a in ("gx", "gy", "gz"))
    me = (gx, gy, gz)

    def dev(d):
        return tuple(lax.rem(m + (q + s), s) for m, q, s in zip(me, d, sizes))

    loads = []
    for f, ref in ((B, b_in), (S, s_in), (FX, fx_in), (FY, fy_in), (FZ, fz_in)):
        c = pltpu.make_async_copy(ref, C.at[f, 0, pl.ds(2, 16), pl.ds(8, 32)], in_sem.at[f])
        c.start()
        loads.append(c)

    far = [(a, b, c) for a in range(GX) for b in (-1, 0, 1) for c in (-1, 0, 1) if (a, b, c) != (0, 0, 0)]
    far = sorted(far, key=lambda d: -(min(d[0], GX - d[0]) + abs(d[1]) + abs(d[2])))
    bar = pltpu.get_barrier_semaphore()
    for d in far:
        pl.semaphore_signal(bar, inc=1, device_id=dev(d), device_id_type=MESH)

    def start(msgs, ss):
        tiles = 0
        for d, src, dst in msgs:
            tiles += math.prod(dst.shape) // 1024
            c = pltpu.make_async_remote_copy(
                src_ref=src, dst_ref=dst, send_sem=sems.at[ss], recv_sem=sems.at[ss + 1],
                device_id=dev(d), device_id_type=MESH)
            c.start()
        return tiles, ss

    def finish(sent):
        tiles, ss = sent
        span = count.at[pl.ds(0, tiles)]
        pltpu.make_async_copy(span, span, sems.at[ss + 1]).wait()
        pltpu.make_async_copy(span, span, sems.at[ss]).wait()

    lane128 = iota((1, 128), 1)
    first = [m == 0 for m in me]
    last = [m == s - 1 for m, s in zip(me, sizes)]

    for c in loads:
        c.wait()

    C[FX, 0, 17, 8:40, :] = jnp.where(last[0], 0.0, C[FX, 0, 17, 8:40, :])
    row8 = iota((8, 128), 0)
    lane32 = iota((32, 128), 1)

    def close(x, _):
        C[FY, 0, x, 32:40, :] = jnp.where(last[1] & (row8 == 7), 0.0, C[FY, 0, x, 32:40, :])
        C[FZ, 0, x, 8:40, :] = jnp.where(last[2] & (lane32 == 127), 0.0, C[FZ, 0, x, 8:40, :])
        return 0

    loop(2, 18, close, 0)

    TILES = ((0, 6), (6, 5), (11, 5))

    for t, (x0, n) in enumerate(TILES):
        def pack(i, acc, x0=x0):
            for f in range(5):
                g = i * 5 + f
                v = pltpu.roll(C[f, 0, 2 + x0 + i, 8:40, :], 4 * g + 2, 1)
                acc = jnp.where((lane32 >> 2) == g, v, acc)
            return acc
        ZC[t] = loop(0, n, pack, jnp.zeros((32, 128), F32))

    pl.semaphore_wait(bar, len(far))

    ROWS = {1: (32, 0, 8), -1: (8, 40, 8), 0: (8, 8, 32)}

    def fine_msgs(xs, stack, ys, yland, zs, zland, es, eland, ztiles):
        msgs = []
        for d in ALL26:
            dx, dy, dz = d
            if dz != 0:
                sy, ty, ny = ROWS[dy]
                side = 0 if dz == 1 else 1
                s0, t0, nt = ztiles[dx]
                msgs.append((d, zs.at[pl.ds(s0, nt), pl.ds(sy - 8, ny)], zland.at[side, pl.ds(t0, nt), pl.ds(ty, ny)]))
            elif dy == 0:
                sx, tx, nx = xs[dx]
                msgs.append((d, stack(pl.ds(sx, nx)), stack(pl.ds(tx, nx))))
            elif dx == 0:
                side = 0 if dy == 1 else 1
                msgs.append((d, ys.at[side], yland.at[side]))
            else:
                e = EDGES.index((dx, dy))
                msgs.append((d, es.at[e], eland.at[e]))
        return msgs

    CUP = [(f, 39, 7) for f in range(5)] + [(FY, 38, 6)]
    CDOWN = [(f, 8, 40) for f in range(5)]
    C2 = C.reshape(5 * 2 * 20 * 48, 128)

    def crows(f, row):
        return pl.ds((2 * f * 20 + 2) * 48 + row, 16, stride=48)

    CY[1, 5] = jnp.zeros((16, 128), F32)
    for side, rows in ((0, CUP), (1, CDOWN)):
        for k, (f, here, _) in enumerate(rows):
            CY[side, k] = C2[crows(f, here), :]

    def cedge(dx, dy):
        x, tx = (17, 1) if dx == 1 else (2, 18)
        y, ty = (39, 7) if dy == 1 else (8, 40)
        rows = [(f, x, y, tx, ty) for f in range(5)]
        if dy == 1:
            rows.append((FY, x, y - 1, tx, ty - 1))
        if dx == 1:
            rows.append((FX, x - 1, y, tx - 1, ty))
        return rows

    for e, (dx, dy) in enumerate(EDGES):
        for k, (f, x, y, _, _) in enumerate(cedge(dx, dy)):
            CE[e, k:k + 1, :] = C[f, 0, x, y:y + 1, :]

    c_msgs = fine_msgs({1: (17, 1, 1), -1: (2, 18, 1)}, lambda xs: C.at[:, 0, xs, pl.ds(8, 32)],
                       CY, CYL, ZC, LC, CE, CEL, {1: (2, 0, 1), 0: (0, 1, 3), -1: (0, 4, 1)})
    c_msgs.append(((1, 0, 0), C.at[FX, 0, pl.ds(16, 1), pl.ds(8, 32)], C.at[FX, 0, pl.ds(0, 1), pl.ds(8, 32)]))
    c_sent = start(c_msgs, 0)

    li, lo = iota((256, 128), 0), iota((256, 128), 1)
    hit = ((li & 127) >> 1) == (lo & 63)
    hit = hit & ((li >> 7) == (lo >> 6))
    odd = (li & 1) == 1
    wa = jnp.where(hit, 1.0 / 16, 0.0)
    wb = jnp.where(li < 128, jnp.where(hit & odd, 1.0 / 16, 0.0), jnp.where(hit, 1.0 / 8, 0.0))

    def mid(i, _):
        x = 2 + 2 * i
        ev, od = pl.ds(8, 16, stride=2), pl.ds(9, 16, stride=2)
        mx = C[FX, 0, x + 1, ev, :] + C[FX, 0, x + 1, od, :]
        my = C[FY, 0, x, od, :] + C[FY, 0, x + 1, od, :]
        mz = (C[FZ, 0, x, ev, :] + C[FZ, 0, x, od, :]) + (C[FZ, 0, x + 1, ev, :] + C[FZ, 0, x + 1, od, :])
        ms = (C[S, 0, x, ev, :] + C[S, 0, x, od, :]) + (C[S, 0, x + 1, ev, :] + C[S, 0, x + 1, od, :])
        RX[0, i, 0:16, :] = mx
        RX[1, i, 0:16, :] = my
        RX[0, i, 16:32, :] = mz
        RX[1, i, 16:32, :] = ms
        return 0

    loop(0, 8, mid, 0)
    for p, w in ((0, wa), (1, wb)):
        lhs = jnp.concatenate(
            [RX[q, :, 16 * p:16 * p + 16, :].reshape(128, 128) for q in (0, 1)], axis=1)
        KP[p, 6:14, 8:24, :] = dot(lhs, w).reshape(8, 16, 128)

    lane16 = iota((16, 128), 1)

    def pack_mid(load, base):
        acc = jnp.zeros((16, 128), F32)
        for x in range(8):
            v = load(x)
            acc = jnp.where((lane16 >> 3) == 2 * x, shift(v, 16 * x - (base + 56), 1), acc)
            acc = jnp.where((lane16 >> 3) == 2 * x + 1, shift(v, 16 * x + 8 - base, 1), acc)
        return acc

    for t in range(2):
        acc = [jnp.zeros((16, 128), F32)] * 2
        for x in range(8):
            for side, edge in ((0, 56), (1, 0)):
                v = shift(KP[t, 6 + x, 8:24, :], 8 * x - edge, 1)
                acc[side] = jnp.where(((lane16 >> 3) & 7) == x, v, acc[side])
        ZK[0, t] = acc[0]
        ZK[1, t] = acc[1]

    MROWS = {1: (16, 0, 8), -1: (8, 24, 8), 0: (8, 8, 16)}

    def mid_msgs(xs, field, zsrc, zland):
        msgs = []
        for d in ALL26:
            dx, dy, dz = d
            sy, ty, ny = MROWS[dy]
            if dz == 0:
                sx, tx, nx = xs[dx]
                msgs.append((d, field(pl.ds(sx, nx), pl.ds(sy, ny)), field(pl.ds(tx, nx), pl.ds(ty, ny))))
            else:
                side = 0 if dz == 1 else 1
                msgs.append((d, zsrc(side, pl.ds(sy - 8, ny)), zland(side, 1 - dx, pl.ds(ty, ny))))
        return msgs

    finish(c_sent)
    for side, rows in ((0, CUP), (1, CDOWN)):
        for k, (f, _, there) in enumerate(rows):
            C2[crows(f, there), :] = CYL[side, k]
    for e, (dx, dy) in enumerate(EDGES):
        for k, (f, _, _, x, y) in enumerate(cedge(dx, dy)):
            C[f, 0, x, y:y + 1, :] = CEL[e, k:k + 1, :]

    lane48 = iota((48, 128), 1)
    for j, (x0, n, i0) in enumerate(((0, 2, 3), (2, 6, 0), (8, 5, 0), (13, 5, 0), (18, 2, 0))):
        both = jnp.where((lane48 & 3) >= 2, LC[1, j], LC[0, j])
        LC[0, j] = both

        def spread(i, _, j=j, x0=x0, i0=i0):
            both = LC[0, j]
            for f in range(5):
                C[f, 1, x0 + i, :, :] = pltpu.roll(both, 126 + 128 - 4 * ((i + i0) * 5 + f), 1)
            return 0

        loop(0, n, spread, 0)

    def ld(ref, x):
        return jnp.concatenate([ref[0, x], ref[1, x]], axis=1)

    def ldc(f, x):
        return jnp.concatenate([C[f, 0, x], C[f, 1, x]], axis=1)

    def st(ref, x, v):
        ref[0, x] = v[:, :128]
        ref[1, x] = v[:, 128:]

    t_inv, ((ca, cb),) = cheb_factors(2, 0.5, 2.0)

    def diag0(x, _):
        fy, fz = ldc(FY, x), ldc(FZ, x)
        diag = (ldc(S, x) + ldc(FX, x) + ldc(FX, x - 1)) + (fy + shift(fy, 1, 0)) + (fz + shift(fz, 1, 1))
        inv = 1.0 / diag
        st(ID, x, inv)
        st(D, x, t_inv * inv * ldc(B, x))
        return 0

    loop(1, 19, diag0, 0, chunks=2)

    def residual0(ref, x):
        v = ld(ref, x)
        gy_ = ldc(FY, x) * (v - shift(v, -1, 0))
        gz_ = ldc(FZ, x) * (v - shift(v, -1, 1))
        av = ldc(S, x) * v + ldc(FX, x) * (v - ld(ref, x + 1)) + ldc(FX, x - 1) * (v - ld(ref, x - 1))
        av = av + (gy_ - shift(gy_, 1, 0)) + (gz_ - shift(gz_, 1, 1))
        return v, ldc(B, x) - av

    def own_residual0(ref, x):
        wide, fy = ref[0, x], C[FY, 0, x]
        flux = fy * (wide - shift(wide, -1, 0))
        av = (flux - shift(flux, 1, 0))[8:40]
        v, side = wide[8:40], ref[1, x, 8:40, :]
        fz = C[FZ, 0, x, 8:40, :]
        low_z = shift(jnp.where(lane32 == 127, C[FZ, 1, x, 8:40, :], fz), 1, 1)
        av = av + fz * (v - shift(jnp.where(lane32 == 0, side, v), -1, 1))
        av = av + low_z * (v - shift(jnp.where(lane32 == 127, side, v), 1, 1))
        av = av + C[FX, 0, x, 8:40, :] * (v - ref[0, x + 1, 8:40, :])
        av = av + C[FX, 0, x - 1, 8:40, :] * (v - ref[0, x - 1, 8:40, :])
        return v, C[B, 0, x, 8:40, :] - (av + C[S, 0, x, 8:40, :] * v)

    def pre0(x, _):
        d, r = own_residual0(D, x)
        V[0, x, 8:40, :] = d + (ca * d + cb * ID[0, x, 8:40, :] * r)
        return 0

    loop(2, 18, pre0, 0, chunks=2)

    def pack_v(i, acc):
        v = pltpu.roll(V[0, 2 + i, 8:40, :], 4 * i + 2, 1)
        return jnp.where((lane32 >> 2) == i, v, acc)

    ZV[0] = loop(0, 16, pack_v, jnp.zeros((32, 128), F32))
    V2 = V.reshape(2 * 20 * 48, 128)

    def vrows(row):
        return pl.ds(2 * 48 + row, 16, stride=48)

    for k in (0, 1):
        VY[0, k] = V2[vrows(38 + k), :]
        VY[1, k] = V2[vrows(8 + k), :]

    def vedge(dx, dy):
        x, tx = (16, 0) if dx == 1 else (2, 18)
        y, ty = (38, 6) if dy == 1 else (8, 40)
        return [(x + a, y + b, tx + a, ty + b) for a in (0, 1) for b in (0, 1)]

    for e, (dx, dy) in enumerate(EDGES):
        for k, (x, y, _, _) in enumerate(vedge(dx, dy)):
            VE[e, k:k + 1, :] = V[0, x, y:y + 1, :]
    v_sent = start(fine_msgs({1: (16, 0, 2), -1: (2, 18, 2)}, lambda xs: V.at[0, xs, pl.ds(8, 32)],
                             VY, VYL, ZV, LV, VE, VEL, {1: (0, 0, 1), 0: (0, 1, 1), -1: (0, 2, 1)}), 2)
    k_sent = start(
        mid_msgs({1: (8, 0, 6), -1: (6, 14, 5), 0: (6, 6, 8)},
                 lambda xs, ys: KP.at[:, xs, ys],
                 lambda side, ys: ZK.at[side, :, ys], lambda side, j, ys: LK.at[side, j, :, ys]), 4)

    wi, wo = iota((128, 128), 0), iota((128, 128), 1)
    in32 = wo < 32

    def packed(rows, w):
        r = dot(rows, w)
        acc = r[0:8]
        for i in range(1, 4):
            acc = acc + shift(r[8 * i:8 * i + 8], 32 * i, 1)
        return acc

    for f, half in ((0, 0), (1, 64), (2, 0), (3, 64)):
        p = f // 2
        rows = []
        for i in range(4):
            x = 6 + 2 * i
            e0, o0 = KP[p, x, pl.ds(8, 8, stride=2), :], KP[p, x, pl.ds(9, 8, stride=2), :]
            e1, o1 = KP[p, x + 1, pl.ds(8, 8, stride=2), :], KP[p, x + 1, pl.ds(9, 8, stride=2), :]
            rows.append((e1 + o1) if f == 0 else (o0 + o1) if f == 1 else (e0 + o0) + (e1 + o1))
        z = wi - half
        sel = (z >= 0) & (z < 64) & ((z >> 1) == wo) & in32
        if f == 2:
            sel = sel & ((z & 1) == 1)
        K2P[f] = packed(jnp.concatenate(rows, 0), jnp.where(sel, 1.0 / (8 if f == 3 else 16), 0.0))
    rim = [C[FY, 0, 2 + x, 7:8, :] for x in range(16)]
    rim = jnp.concatenate(
        [jnp.broadcast_to((rim[4 * i] + rim[4 * i + 1]) + (rim[4 * i + 2] + rim[4 * i + 3]), (8, 128)) for i in range(4)], 0)
    below = packed(rim, jnp.where(((wi >> 2) == wo) & in32, 1.0 / 256, 0.0))
    K2P[4] = jnp.where(row8 == 0, below, shift(K2P[1], 1, 0))

    def nk(d):
        return 5 if d[1] == 1 else 4

    def far_msgs(src, land):
        return [(d, src(d), land(d, gx, 1 - d[2], pl.ds(8 - 8 * d[1], 8))) for d in far]

    LK2[gx, 1, :, 8:16, :] = K2P[...]

    finish(v_sent)
    for k in (0, 1):
        V2[vrows(6 + k), :] = VYL[0, k]
        V2[vrows(40 + k), :] = VYL[1, k]
    for e, (dx, dy) in enumerate(EDGES):
        for k, (_, _, x, y) in enumerate(vedge(dx, dy)):
            V[0, x, y:y + 1, :] = VEL[e, k:k + 1, :]
    for j, (x0, n, i0) in enumerate(((0, 2, 14), (2, 16, 0), (18, 2, 0))):
        LV[0, j] = jnp.where((lane48 & 3) >= 2, LV[1, j], LV[0, j])

        def spread_v(i, _, j=j, x0=x0, i0=i0):
            V[1, x0 + i, :, :] = pltpu.roll(LV[0, j], 126 + 128 - 4 * (i + i0), 1)
            return 0

        loop(0, n, spread_v, 0)

    r48, l256 = iota((48, 256), 0), iota((48, 256), 1)
    keep0 = ((r48 >= jnp.where(first[1], 8, 7)) & (r48 < jnp.where(last[1], 40, 41))
             & ((l256 < jnp.where(last[2], 128, 129)) | (l256 > jnp.where(first[2], 255, 254))))

    def res0(x, _):
        _, r = residual0(V, x)
        inside = ((x > 1) | jnp.logical_not(first[0])) & ((x < 18) | jnp.logical_not(last[0]))
        st(D, x, jnp.where(keep0 & inside, r, 0.0))
        return 0

    loop(1, 19, res0, 0, chunks=2)

    def rest0(i, _):
        x = 2 + 2 * i
        v = 0.125 * (ld(D, x - 1) + ld(D, x + 2)) + 0.375 * (ld(D, x) + ld(D, x + 1))
        st(RX, i, v)
        for h in (0, 1):
            rows = [RX[h, i, pl.ds(7 + k, 16, stride=2), :] for k in range(4)]
            RX[h, i, 0:16, :] = 0.125 * (rows[0] + rows[3]) + 0.375 * (rows[1] + rows[2])
        return 0

    loop(0, 8, rest0, 0)
    zin = jnp.where(li < 192, li, li - 256)
    wr = restrict_weights(zin, lo - 32, (lo >= 32) & (lo < 96))
    lhs = jnp.concatenate([RX[h, :, 0:16, :].reshape(128, 128) for h in (0, 1)], axis=1)
    B1[6:14, 8:24, :] = dot(lhs, wr).reshape(8, 16, 128)
    ZB[...] = pack_mid(lambda x: B1[6 + x, 8:24, :], 32)
    b_sent = start(
        mid_msgs({1: (9, 1, 5), -1: (6, 14, 5), 0: (6, 6, 8)},
                 lambda xs, ys: B1.at[xs, ys],
                 lambda side, ys: ZB.at[ys], lambda side, j, ys: LB.at[side, j, ys]), 6)

    k2_sent = start(far_msgs(lambda d: K2P.at[pl.ds(0, nk(d))], lambda d, g, j, ys: LK2.at[g, j, pl.ds(0, nk(d)), ys]), 8)

    finish(k_sent)
    lane32r = iota((32, 128), 1)

    def z_halo(lm, lp, own, q):
        low = pltpu.roll(lm, 24 + 128 - 16 * q, 1)
        high = pltpu.roll(lp, 88 + 128 - 16 * q, 1)
        return jnp.where(lane32r < 32, low, jnp.where(lane32r < 96, own, high))

    MID = ((0, 0, 6, 2), (1, 6, 8, 0), (2, 14, 5, 0))
    for j, x0, n, i0 in MID:
        def spread_k(i, _, j=j, x0=x0, i0=i0):
            for f in range(4):
                own = pltpu.roll(KP[f // 2, x0 + i], 32 if f % 2 == 0 else 96, 1)
                at = 8 * (i + i0) + 64 * (f % 2)
                low, high = shift(LK[0, j, f // 2], 24 - at, 1), shift(LK[1, j, f // 2], 96 - at, 1)
                K1[f, x0 + i] = jnp.where(lane32r < 32, low, jnp.where(lane32r < 96, own, high))
            return 0

        loop(0, n, spread_k, 0)

    def diag1(x, _):
        fy, fz = K1[1, x], K1[2, x]
        diag = (K1[3, x] + K1[0, x] + K1[0, x - 1]) + (fy + shift(fy, 1, 0)) + (fz + shift(fz, 1, 1))
        I1[x] = 1.0 / diag
        return 0

    loop(1, 19, diag1, 0)

    finish(b_sent)
    for j, x0, n, i0 in ((0, 1, 5, 3), (1, 6, 8, 0), (2, 14, 5, 0)):
        def spread_b(i, _, j=j, x0=x0, i0=i0):
            b = z_halo(LB[0, j], LB[1, j], B1[x0 + i], i + i0)
            B1[x0 + i] = b
            D1[x0 + i] = t_inv * I1[x0 + i] * b
            return 0

        loop(0, n, spread_b, 0)

    def residual(K, ref, b, x, xp, xm, low_y=None):
        v = ref[x]
        fy, fz = K[1, x], K[2, x]
        gz_ = fz * (v - shift(v, -1, 1))
        av = K[3, x] * v + K[0, x] * (v - ref[xp]) + K[0, xm] * (v - ref[xm])
        if low_y is None:
            gy_ = fy * (v - shift(v, -1, 0))
            av = av + (gy_ - shift(gy_, 1, 0))
        else:
            av = av + fy * (v - shift(v, -1, 0)) + low_y * (v - shift(v, 1, 0))
        av = av + (gz_ - shift(gz_, 1, 1))
        return v, b[x] - av

    def pre1(x, _):
        d, r = residual(K1, D1, B1, x, x + 1, x - 1)
        X1[x] = d + (ca * d + cb * I1[x] * r)
        return 0

    loop(2, 18, pre1, 0)

    r32 = iota((32, 128), 0)
    keep1 = ((r32 >= jnp.where(first[1], 8, 7)) & (r32 < jnp.where(last[1], 24, 25))
             & (lane32r >= jnp.where(first[2], 32, 31)) & (lane32r < jnp.where(last[2], 96, 97)))

    def res1(x, _):
        _, r = residual(K1, X1, B1, x, x + 1, x - 1)
        inside = ((x > 5) | jnp.logical_not(first[0])) & ((x < 14) | jnp.logical_not(last[0]))
        D1[x] = jnp.where(keep1 & inside, r, 0.0)
        return 0

    loop(5, 15, res1, 0)

    rows = []
    for i in range(4):
        x = 6 + 2 * i
        RX1[i] = 0.125 * (D1[x - 1] + D1[x + 2]) + 0.375 * (D1[x] + D1[x + 1])
        parts = [RX1[i, pl.ds(7 + k, 8, stride=2), :] for k in range(4)]
        rows.append(0.125 * (parts[0] + parts[3]) + 0.375 * (parts[1] + parts[2]))
    B2P[...] = packed(jnp.concatenate(rows, 0), restrict_weights(wi - 32, wo, in32))
    b2_sent = start(far_msgs(lambda d: B2P, lambda d, g, j, ys: LB2.at[g, j, ys]), 10)
    LB2[gx, 1, 8:16, :] = B2P[...]

    NX2 = 4 * GX
    finish(k2_sent)
    lane24 = iota((24, 128), 1)

    def unpack2(lm, lc, lp, i):
        return jnp.where(lane24 < 32, pltpu.roll(lm, 128 - 32 * i, 1),
                         jnp.where(lane24 < 64, pltpu.roll(lc, 160 - 32 * i, 1), pltpu.roll(lp, 192 - 32 * i, 1)))

    def spread_k2(x, _):
        g, i = x >> 2, x & 3
        k2 = [unpack2(LK2[g, 0, f], LK2[g, 1, f], LK2[g, 2, f], i) for f in range(5)]
        for f in range(4):
            K2[f, x] = k2[f]
        K2[4, x] = jnp.where(iota((24, 128), 0) < 8, k2[4], shift(k2[1], 1, 0))
        return 0

    loop(0, NX2, spread_k2, 0)

    def up(x):
        return lax.rem(x + 1, NX2)

    def down(x):
        return lax.rem(x + (NX2 - 1), NX2)

    def diag2(x, _):
        fz = K2[2, x]
        diag = (K2[3, x] + K2[0, x] + K2[0, down(x)]) + (K2[1, x] + K2[4, x]) + (fz + shift(fz, 1, 1))
        I2[x] = 1.0 / diag
        return 0

    loop(0, NX2, diag2, 0)

    t2_inv, factors2 = cheb_factors(6, 0.05, 2.0)
    finish(b2_sent)

    def spread_b2(x, _):
        g, i = x >> 2, x & 3
        b = unpack2(LB2[g, 0], LB2[g, 1], LB2[g, 2], i)
        Y2[x] = b
        d = t2_inv * I2[x] * b
        D2[x] = d
        X2[0, x] = d
        return 0

    loop(0, NX2, spread_b2, 0)

    r24 = iota((24, 128), 0)
    keep2 = ((r24 >= jnp.where(first[1], 8, 4)) & (r24 < jnp.where(last[1], 16, 20))
             & (lane24 >= jnp.where(first[2], 32, 24)) & (lane24 < jnp.where(last[2], 64, 72)))
    for n, (fa, fb) in enumerate(factors2):
        src, dst = X2.at[n % 2], X2.at[1 - n % 2]
        final = n == len(factors2) - 1

        def step(x, _, src=src, dst=dst, fa=fa, fb=fb, final=final):
            v, r = residual(K2, src, Y2, x, up(x), down(x), K2[4, x])
            d = fa * D2[x] + fb * I2[x] * r
            if final:
                dst[x] = jnp.where(keep2, v + d, 0.0)
            else:
                D2[x] = d
                dst[x] = v + d
            return 0

        loop(0, NX2, step, 0)
    x2 = X2.at[len(factors2) % 2]

    wp = prolong_weights(wi - 32, wo - 32)
    z1 = dot(x2[...].reshape(NX2 * 24, 128), wp).reshape(NX2, 24, 128)
    Y2[...] = z1

    def pro_y1(x, _):
        c = Y2[x]
        lower, upper = shift(c, 1, 0), shift(c, -1, 0)
        PY1[x, pl.ds(0, 16, stride=2), :] = (0.75 * c + 0.25 * lower)[4:20]
        PY1[x, pl.ds(1, 16, stride=2), :] = (0.75 * c + 0.25 * upper)[4:20]
        return 0

    loop(0, NX2, pro_y1, 0)

    def pro_x1(i, _):
        a = 4 * gx + (i - 3)

        def slab(k):
            return jnp.where((k >= 0) & (k < NX2), PY1[lax.rem(k + NX2, NX2)], 0.0)

        c = 0.75 * slab(a)
        X1[2 * i] = X1[2 * i] + (c + 0.25 * slab(a - 1))
        X1[2 * i + 1] = X1[2 * i + 1] + (c + 0.25 * slab(a + 1))
        return 0

    loop(1, 9, pro_x1, 0)

    def post1(x, _):
        v, r = residual(K1, X1, B1, x, x + 1, x - 1)
        d = t_inv * I1[x] * r
        D1[x] = d
        T1[x] = v + d
        return 0

    loop(3, 17, post1, 0)
    keep1p = ((r32 >= jnp.where(first[1], 8, 4)) & (r32 < jnp.where(last[1], 24, 28))
              & (lane32r >= jnp.where(first[2], 32, 28)) & (lane32r < jnp.where(last[2], 96, 100)))

    def post1b(x, _):
        v, r = residual(K1, T1, B1, x, x + 1, x - 1)
        inside = ((x > 5) | jnp.logical_not(first[0])) & ((x < 14) | jnp.logical_not(last[0]))
        X1[x] = jnp.where(keep1p & inside, v + (ca * D1[x] + cb * I1[x] * r), 0.0)
        return 0

    loop(4, 16, post1b, 0)

    pi, po = iota((128, 256), 0), iota((128, 256), 1)
    wq = prolong_weights(pi - 32, jnp.where(po < 192, po, po - 256))
    for i in range(12):
        z0 = dot(X1[4 + i], wq)
        lower, upper = shift(z0, 1, 0), shift(z0, -1, 0)
        ev, od = 0.75 * z0 + 0.25 * lower, 0.75 * z0 + 0.25 * upper
        for h in (0, 1):
            PY0[h, i, pl.ds(0, 24, stride=2), :] = ev[4:28, 128 * h:128 * h + 128]
            PY0[h, i, pl.ds(1, 24, stride=2), :] = od[4:28, 128 * h:128 * h + 128]

    def pro_x0(i, _):
        c = 0.75 * ld(PY0, i + 1)
        st(V, 2 * i, ld(V, 2 * i) + (c + 0.25 * ld(PY0, i)))
        st(V, 2 * i + 1, ld(V, 2 * i + 1) + (c + 0.25 * ld(PY0, i + 2)))
        return 0

    loop(0, 10, pro_x0, 0)

    def post0(x, _):
        v, r = residual0(V, x)
        d = t_inv * ld(ID, x) * r
        st(D, x, d)
        st(W, x, v + d)
        return 0

    loop(1, 19, post0, 0, chunks=2)

    def post0b(x, _):
        v, r = own_residual0(W, x)
        out[x - 2] = v + (ca * D[0, x, 8:40, :] + cb * ID[0, x, 8:40, :] * r)
        return 0

    loop(2, 18, post0b, 0, chunks=2)


def solution(mesh):
    sizes = tuple(mesh.shape[a] for a in ("gx", "gy", "gz"))
    nx2 = 4 * sizes[0]

    def vm(*shape):
        return pltpu.VMEM(shape, F32)

    dma = lambda n: pltpu.SemaphoreType.DMA((n,))
    scratch = [
        vm(5, 2, 20, 48, 128), vm(2, 20, 48, 128), vm(2, 20, 48, 128), vm(2, 20, 48, 128), vm(2, 20, 48, 128),
        vm(2, 8, 48, 128), vm(3, 32, 128), vm(2, 5, 48, 128), vm(1, 32, 128), vm(2, 3, 48, 128),
        vm(2, 20, 32, 128), vm(4, 20, 32, 128), vm(2, 2, 16, 128), vm(2, 3, 2, 32, 128),
        vm(20, 32, 128), vm(20, 32, 128), vm(20, 32, 128), vm(20, 32, 128), vm(20, 32, 128),
        vm(16, 128), vm(2, 3, 32, 128), vm(4, 32, 128),
        vm(5, 8, 128), vm(sizes[0], 3, 5, 24, 128), vm(8, 128), vm(sizes[0], 3, 24, 128),
        vm(5, nx2, 24, 128), vm(nx2, 24, 128), vm(2, nx2, 24, 128), vm(nx2, 24, 128), vm(nx2, 24, 128),
        vm(nx2, 32, 128), vm(2, 12, 48, 128),
        vm(2, 6, 16, 128), vm(2, 6, 16, 128), vm(4, 8, 128), vm(4, 8, 128),
        vm(2, 2, 16, 128), vm(2, 2, 16, 128), vm(4, 8, 128), vm(4, 8, 128),
        vm(512, 8, 128), dma(5), dma(12),
    ]

    def local(right_side, face_x, face_y, face_z, absorb):
        return pl.pallas_call(
            functools.partial(kernel, sizes),
            out_shape=jax.ShapeDtypeStruct(right_side.shape, F32),
            in_specs=[pl.BlockSpec(memory_space=pltpu.HBM)] * 5,
            out_specs=pl.BlockSpec(memory_space=pltpu.VMEM),
            scratch_shapes=scratch,
            compiler_params=pltpu.CompilerParams(
                collective_id=0, has_side_effects=True, vmem_limit_bytes=62 * 1024 * 1024),
            name="vcycle",
        )(right_side, face_x, face_y, face_z, absorb)

    spec = P("gx", "gy", "gz")
    return jax.shard_map(local, mesh=mesh, in_specs=(spec,) * 5, out_specs=spec, check_vma=False)
```

```python
import functools
import math

import jax
import jax.numpy as jnp
from jax import lax
from jax.experimental import pallas as pl
from jax.experimental.pallas import tpu as pltpu
from jax.sharding import PartitionSpec as P

MESH = pl.DeviceIdType.MESH
F32 = jnp.float32
HI = lax.Precision.HIGHEST

B, S, FY, FZ, FX = range(5)

ALL26 = sorted(
    [(a, b, c) for a in (-1, 0, 1) for b in (-1, 0, 1) for c in (-1, 0, 1) if (a, b, c) != (0, 0, 0)],
    key=lambda d: -sum(map(abs, d)),
)


def cheb_factors(steps, lowest, highest):
    centre = 0.5 * (lowest + highest)
    half = 0.5 * (highest - lowest)
    q = centre / half
    rho = 1.0 / q
    out = []
    for _ in range(steps - 1):
        nxt = 1.0 / (2.0 * q - rho)
        out.append((nxt * rho, 2.0 * nxt / half))
        rho = nxt
    return 1.0 / centre, out


EDGES = [(1, 1), (1, -1), (-1, 1), (-1, -1)]


def iota(shape, dim):
    return lax.broadcasted_iota(jnp.int32, shape, dim)


def dot(a, b):
    return jnp.dot(a, b, precision=HI, preferred_element_type=F32)


def shift(v, amount, axis):
    return pltpu.roll(v, amount % v.shape[axis], axis)


def restrict_weights(z, k, ok):
    t = z - 2 * k
    w = jnp.where((t == 0) | (t == 1), 0.375, jnp.where((t == -1) | (t == 2), 0.125, 0.0))
    return jnp.where(ok, w, 0.0)


def prolong_weights(coarse, fine):
    k = fine >> 1
    side = jnp.where((fine & 1) == 0, k - 1, k + 1)
    return jnp.where(coarse == k, 0.75, jnp.where(coarse == side, 0.25, 0.0))


def loop(lo, hi, body, init=0, chunks=1):
    u = (hi - lo) // chunks
    if chunks == 1:
        for i in range(lo, hi):
            init = body(i, init)
        return init

    def chunk(c, carry):
        for k in range(u):
            carry = body(lo + c * u + k, carry)
        return carry

    return lax.fori_loop(0, chunks, chunk, init)


def kernel(sizes, b_in, fx_in, fy_in, fz_in, s_in, out,
           C, ID, V, D, W, RX, ZC, LC, ZV, LV,
           KP, K1, ZK, LK, B1, I1, X1, D1, T1, ZB, LB, RX1,
           K2P, LK2, K2Z, LK2Z, B2P, LB2, K2, I2, X2, D2, Y2, PY1, PY0,
           CY, CYL, CE, CEL, VY, VYL, VE, VEL, count, in_sem, sems):
    GX, GY, GZ = sizes
    gx, gy, gz = (lax.axis_index(a) for a in ("gx", "gy", "gz"))
    me = (gx, gy, gz)

    def dev(d):
        return tuple(lax.rem(m + (q + s), s) for m, q, s in zip(me, d, sizes))

    loads = []
    for f, ref in ((B, b_in), (S, s_in), (FX, fx_in), (FY, fy_in), (FZ, fz_in)):
        c = pltpu.make_async_copy(ref, C.at[f, 0, pl.ds(2, 16), pl.ds(8, 32)], in_sem.at[f])
        c.start()
        loads.append(c)

    far = [(a, b, c) for a in range(GX) for b in (-1, 0, 1) for c in (-1, 0, 1) if (a, b, c) != (0, 0, 0)]
    far = sorted(far, key=lambda d: -(min(d[0], GX - d[0]) + abs(d[1]) + abs(d[2])))
    bar = pltpu.get_barrier_semaphore()
    for d in far:
        pl.semaphore_signal(bar, inc=1, device_id=dev(d), device_id_type=MESH)

    def start(msgs, ss):
        tiles = 0
        for d, src, dst in msgs:
            tiles += math.prod(dst.shape) // 1024
            c = pltpu.make_async_remote_copy(
                src_ref=src, dst_ref=dst, send_sem=sems.at[ss], recv_sem=sems.at[ss + 1],
                device_id=dev(d), device_id_type=MESH)
            c.start()
        return tiles, ss

    def finish(sent):
        tiles, ss = sent
        span = count.at[pl.ds(0, tiles)]
        pltpu.make_async_copy(span, span, sems.at[ss + 1]).wait()
        pltpu.make_async_copy(span, span, sems.at[ss]).wait()

    lane128 = iota((1, 128), 1)
    first = [m == 0 for m in me]
    last = [m == s - 1 for m, s in zip(me, sizes)]

    for c in loads:
        c.wait()

    C[FX, 0, 17, 8:40, :] = jnp.where(last[0], 0.0, C[FX, 0, 17, 8:40, :])
    row8 = iota((8, 128), 0)
    lane32 = iota((32, 128), 1)

    def close(x, _):
        C[FY, 0, x, 32:40, :] = jnp.where(last[1] & (row8 == 7), 0.0, C[FY, 0, x, 32:40, :])
        C[FZ, 0, x, 8:40, :] = jnp.where(last[2] & (lane32 == 127), 0.0, C[FZ, 0, x, 8:40, :])
        return 0

    loop(2, 18, close, 0)

    TILES = ((0, 6), (6, 5), (11, 5))

    for t, (x0, n) in enumerate(TILES):
        def pack(i, acc, x0=x0):
            for f in range(5):
                g = i * 5 + f
                v = pltpu.roll(C[f, 0, 2 + x0 + i, 8:40, :], 4 * g + 2, 1)
                acc = jnp.where((lane32 >> 2) == g, v, acc)
            return acc
        ZC[t] = loop(0, n, pack, jnp.zeros((32, 128), F32))

    pl.semaphore_wait(bar, len(far))

    ROWS = {1: (32, 0, 8), -1: (8, 40, 8), 0: (8, 8, 32)}

    def fine_msgs(xs, stack, ys, yland, zs, zland, es, eland, ztiles):
        msgs = []
        for d in ALL26:
            dx, dy, dz = d
            if dz != 0:
                sy, ty, ny = ROWS[dy]
                side = 0 if dz == 1 else 1
                s0, t0, nt = ztiles[dx]
                msgs.append((d, zs.at[pl.ds(s0, nt), pl.ds(sy - 8, ny)], zland.at[side, pl.ds(t0, nt), pl.ds(ty, ny)]))
            elif dy == 0:
                sx, tx, nx = xs[dx]
                msgs.append((d, stack(pl.ds(sx, nx)), stack(pl.ds(tx, nx))))
            elif dx == 0:
                side = 0 if dy == 1 else 1
                msgs.append((d, ys.at[side], yland.at[side]))
            else:
                e = EDGES.index((dx, dy))
                msgs.append((d, es.at[e], eland.at[e]))
        return msgs

    CUP = [(f, 39, 7) for f in range(5)] + [(FY, 38, 6)]
    CDOWN = [(f, 8, 40) for f in range(5)]
    C2 = C.reshape(5 * 2 * 20 * 48, 128)

    def crows(f, row):
        return pl.ds((2 * f * 20 + 2) * 48 + row, 16, stride=48)

    CY[1, 5] = jnp.zeros((16, 128), F32)
    for side, rows in ((0, CUP), (1, CDOWN)):
        for k, (f, here, _) in enumerate(rows):
            CY[side, k] = C2[crows(f, here), :]

    def cedge(dx, dy):
        x, tx = (17, 1) if dx == 1 else (2, 18)
        y, ty = (39, 7) if dy == 1 else (8, 40)
        rows = [(f, x, y, tx, ty) for f in range(5)]
        if dy == 1:
            rows.append((FY, x, y - 1, tx, ty - 1))
        if dx == 1:
            rows.append((FX, x - 1, y, tx - 1, ty))
        return rows

    for e, (dx, dy) in enumerate(EDGES):
        for k, (f, x, y, _, _) in enumerate(cedge(dx, dy)):
            CE[e, k:k + 1, :] = C[f, 0, x, y:y + 1, :]

    c_msgs = fine_msgs({1: (17, 1, 1), -1: (2, 18, 1)}, lambda xs: C.at[:, 0, xs, pl.ds(8, 32)],
                       CY, CYL, ZC, LC, CE, CEL, {1: (2, 0, 1), 0: (0, 1, 3), -1: (0, 4, 1)})
    c_msgs.append(((1, 0, 0), C.at[FX, 0, pl.ds(16, 1), pl.ds(8, 32)], C.at[FX, 0, pl.ds(0, 1), pl.ds(8, 32)]))
    c_sent = start(c_msgs, 0)

    li, lo = iota((256, 128), 0), iota((256, 128), 1)
    hit = ((li & 127) >> 1) == (lo & 63)
    hit = hit & ((li >> 7) == (lo >> 6))
    odd = (li & 1) == 1
    wa = jnp.where(hit, 1.0 / 16, 0.0)
    wb = jnp.where(li < 128, jnp.where(hit & odd, 1.0 / 16, 0.0), jnp.where(hit, 1.0 / 8, 0.0))

    def mid(i, _):
        x = 2 + 2 * i
        ev, od = pl.ds(8, 16, stride=2), pl.ds(9, 16, stride=2)
        mx = C[FX, 0, x + 1, ev, :] + C[FX, 0, x + 1, od, :]
        my = C[FY, 0, x, od, :] + C[FY, 0, x + 1, od, :]
        mz = (C[FZ, 0, x, ev, :] + C[FZ, 0, x, od, :]) + (C[FZ, 0, x + 1, ev, :] + C[FZ, 0, x + 1, od, :])
        ms = (C[S, 0, x, ev, :] + C[S, 0, x, od, :]) + (C[S, 0, x + 1, ev, :] + C[S, 0, x + 1, od, :])
        RX[0, i, 0:16, :] = mx
        RX[1, i, 0:16, :] = my
        RX[0, i, 16:32, :] = mz
        RX[1, i, 16:32, :] = ms
        return 0

    loop(0, 8, mid, 0)
    for p, w in ((0, wa), (1, wb)):
        lhs = jnp.concatenate(
            [RX[q, :, 16 * p:16 * p + 16, :].reshape(128, 128) for q in (0, 1)], axis=1)
        KP[p, 6:14, 8:24, :] = dot(lhs, w).reshape(8, 16, 128)

    lane16 = iota((16, 128), 1)

    def pack_mid(load, base):
        acc = jnp.zeros((16, 128), F32)
        for x in range(8):
            v = load(x)
            acc = jnp.where((lane16 >> 3) == 2 * x, shift(v, 16 * x - (base + 56), 1), acc)
            acc = jnp.where((lane16 >> 3) == 2 * x + 1, shift(v, 16 * x + 8 - base, 1), acc)
        return acc

    for t in range(2):
        acc = [jnp.zeros((16, 128), F32)] * 2
        for x in range(8):
            for side, edge in ((0, 56), (1, 0)):
                v = shift(KP[t, 6 + x, 8:24, :], 8 * x - edge, 1)
                acc[side] = jnp.where(((lane16 >> 3) & 7) == x, v, acc[side])
        ZK[0, t] = acc[0]
        ZK[1, t] = acc[1]

    MROWS = {1: (16, 0, 8), -1: (8, 24, 8), 0: (8, 8, 16)}

    def mid_msgs(xs, field, zsrc, zland):
        msgs = []
        for d in ALL26:
            dx, dy, dz = d
            sy, ty, ny = MROWS[dy]
            if dz == 0:
                sx, tx, nx = xs[dx]
                msgs.append((d, field(pl.ds(sx, nx), pl.ds(sy, ny)), field(pl.ds(tx, nx), pl.ds(ty, ny))))
            else:
                side = 0 if dz == 1 else 1
                msgs.append((d, zsrc(side, pl.ds(sy - 8, ny)), zland(side, 1 - dx, pl.ds(ty, ny))))
        return msgs

    finish(c_sent)
    for side, rows in ((0, CUP), (1, CDOWN)):
        for k, (f, _, there) in enumerate(rows):
            C2[crows(f, there), :] = CYL[side, k]
    for e, (dx, dy) in enumerate(EDGES):
        for k, (f, _, _, x, y) in enumerate(cedge(dx, dy)):
            C[f, 0, x, y:y + 1, :] = CEL[e, k:k + 1, :]

    lane48 = iota((48, 128), 1)
    for j, (x0, n, i0) in enumerate(((0, 2, 3), (2, 6, 0), (8, 5, 0), (13, 5, 0), (18, 2, 0))):
        both = jnp.where((lane48 & 3) >= 2, LC[1, j], LC[0, j])
        LC[0, j] = both

        def spread(i, _, j=j, x0=x0, i0=i0):
            both = LC[0, j]
            for f in range(5):
                C[f, 1, x0 + i, :, :] = pltpu.roll(both, 126 + 128 - 4 * ((i + i0) * 5 + f), 1)
            return 0

        loop(0, n, spread, 0)

    def ld(ref, x):
        return jnp.concatenate([ref[0, x], ref[1, x]], axis=1)

    def ldc(f, x):
        return jnp.concatenate([C[f, 0, x], C[f, 1, x]], axis=1)

    def st(ref, x, v):
        ref[0, x] = v[:, :128]
        ref[1, x] = v[:, 128:]

    t_inv, ((ca, cb),) = cheb_factors(2, 0.5, 2.0)

    def diag0(x, _):
        fy, fz = ldc(FY, x), ldc(FZ, x)
        diag = (ldc(S, x) + ldc(FX, x) + ldc(FX, x - 1)) + (fy + shift(fy, 1, 0)) + (fz + shift(fz, 1, 1))
        inv = 1.0 / diag
        st(ID, x, inv)
        st(D, x, t_inv * inv * ldc(B, x))
        return 0

    loop(1, 19, diag0, 0, chunks=2)

    def residual0(ref, x):
        v = ld(ref, x)
        gy_ = ldc(FY, x) * (v - shift(v, -1, 0))
        gz_ = ldc(FZ, x) * (v - shift(v, -1, 1))
        av = ldc(S, x) * v + ldc(FX, x) * (v - ld(ref, x + 1)) + ldc(FX, x - 1) * (v - ld(ref, x - 1))
        av = av + (gy_ - shift(gy_, 1, 0)) + (gz_ - shift(gz_, 1, 1))
        return v, ldc(B, x) - av

    def own_residual0(ref, x):
        wide, fy = ref[0, x], C[FY, 0, x]
        flux = fy * (wide - shift(wide, -1, 0))
        av = (flux - shift(flux, 1, 0))[8:40]
        v, side = wide[8:40], ref[1, x, 8:40, :]
        fz = C[FZ, 0, x, 8:40, :]
        low_z = shift(jnp.where(lane32 == 127, C[FZ, 1, x, 8:40, :], fz), 1, 1)
        av = av + fz * (v - shift(jnp.where(lane32 == 0, side, v), -1, 1))
        av = av + low_z * (v - shift(jnp.where(lane32 == 127, side, v), 1, 1))
        av = av + C[FX, 0, x, 8:40, :] * (v - ref[0, x + 1, 8:40, :])
        av = av + C[FX, 0, x - 1, 8:40, :] * (v - ref[0, x - 1, 8:40, :])
        return v, C[B, 0, x, 8:40, :] - (av + C[S, 0, x, 8:40, :] * v)

    def pre0(x, _):
        d, r = own_residual0(D, x)
        V[0, x, 8:40, :] = d + (ca * d + cb * ID[0, x, 8:40, :] * r)
        return 0

    loop(2, 18, pre0, 0, chunks=2)

    def pack_v(i, acc):
        v = pltpu.roll(V[0, 2 + i, 8:40, :], 4 * i + 2, 1)
        return jnp.where((lane32 >> 2) == i, v, acc)

    ZV[0] = loop(0, 16, pack_v, jnp.zeros((32, 128), F32))
    V2 = V.reshape(2 * 20 * 48, 128)

    def vrows(row):
        return pl.ds(2 * 48 + row, 16, stride=48)

    for k in (0, 1):
        VY[0, k] = V2[vrows(38 + k), :]
        VY[1, k] = V2[vrows(8 + k), :]

    def vedge(dx, dy):
        x, tx = (16, 0) if dx == 1 else (2, 18)
        y, ty = (38, 6) if dy == 1 else (8, 40)
        return [(x + a, y + b, tx + a, ty + b) for a in (0, 1) for b in (0, 1)]

    for e, (dx, dy) in enumerate(EDGES):
        for k, (x, y, _, _) in enumerate(vedge(dx, dy)):
            VE[e, k:k + 1, :] = V[0, x, y:y + 1, :]
    v_sent = start(fine_msgs({1: (16, 0, 2), -1: (2, 18, 2)}, lambda xs: V.at[0, xs, pl.ds(8, 32)],
                             VY, VYL, ZV, LV, VE, VEL, {1: (0, 0, 1), 0: (0, 1, 1), -1: (0, 2, 1)}), 2)
    k_sent = start(
        mid_msgs({1: (8, 0, 6), -1: (6, 14, 5), 0: (6, 6, 8)},
                 lambda xs, ys: KP.at[:, xs, ys],
                 lambda side, ys: ZK.at[side, :, ys], lambda side, j, ys: LK.at[side, j, :, ys]), 4)

    wi, wo = iota((128, 128), 0), iota((128, 128), 1)
    in32 = wo < 32

    def packed(rows, w):
        r = dot(rows, w)
        acc = r[0:8]
        for i in range(1, 4):
            acc = acc + shift(r[8 * i:8 * i + 8], 32 * i, 1)
        return acc

    for f, half in ((0, 0), (1, 64), (2, 0), (3, 64)):
        p = f // 2
        rows = []
        for i in range(4):
            x = 6 + 2 * i
            e0, o0 = KP[p, x, pl.ds(8, 8, stride=2), :], KP[p, x, pl.ds(9, 8, stride=2), :]
            e1, o1 = KP[p, x + 1, pl.ds(8, 8, stride=2), :], KP[p, x + 1, pl.ds(9, 8, stride=2), :]
            rows.append((e1 + o1) if f == 0 else (o0 + o1) if f == 1 else (e0 + o0) + (e1 + o1))
        z = wi - half
        sel = (z >= 0) & (z < 64) & ((z >> 1) == wo) & in32
        if f == 2:
            sel = sel & ((z & 1) == 1)
        K2P[f] = packed(jnp.concatenate(rows, 0), jnp.where(sel, 1.0 / (8 if f == 3 else 16), 0.0))
    rim = [C[FY, 0, 2 + x, 7:8, :] for x in range(16)]
    rim = jnp.concatenate(
        [jnp.broadcast_to((rim[4 * i] + rim[4 * i + 1]) + (rim[4 * i + 2] + rim[4 * i + 3]), (8, 128)) for i in range(4)], 0)
    below = packed(rim, jnp.where(((wi >> 2) == wo) & in32, 1.0 / 256, 0.0))
    K2P[4] = jnp.where(row8 == 0, below, shift(K2P[1], 1, 0))

    def nk(d):
        return 5 if d[1] == 1 else 4

    def far_msgs(src, land):
        return [(d, src(d), land(d, gx, 1 - d[2], pl.ds(8 - 8 * d[1], 8))) for d in far]

    LK2[gx, :, 8:16, :] = K2P[...]

    lane8 = iota((8, 128), 1)

    def spot(f, i):
        g = 4 * f + i
        return g // 10, 12 * (g % 10)

    for side, edge in ((0, 20), (1, 0)):
        acc = [jnp.zeros((8, 128), F32)] * 2
        for f in range(5):
            for i in range(4):
                t, at = spot(f, i)
                v = shift(K2P[f], at - 32 * i - edge, 1)
                acc[t] = jnp.where((lane8 >= at) & (lane8 < at + 12), v, acc[t])
        K2Z[side, 0] = acc[0]
        K2Z[side, 1] = acc[1]

    finish(v_sent)
    for k in (0, 1):
        V2[vrows(6 + k), :] = VYL[0, k]
        V2[vrows(40 + k), :] = VYL[1, k]
    for e, (dx, dy) in enumerate(EDGES):
        for k, (_, _, x, y) in enumerate(vedge(dx, dy)):
            V[0, x, y:y + 1, :] = VEL[e, k:k + 1, :]
    for j, (x0, n, i0) in enumerate(((0, 2, 14), (2, 16, 0), (18, 2, 0))):
        LV[0, j] = jnp.where((lane48 & 3) >= 2, LV[1, j], LV[0, j])

        def spread_v(i, _, j=j, x0=x0, i0=i0):
            V[1, x0 + i, :, :] = pltpu.roll(LV[0, j], 126 + 128 - 4 * (i + i0), 1)
            return 0

        loop(0, n, spread_v, 0)

    r48, l256 = iota((48, 256), 0), iota((48, 256), 1)
    keep0 = ((r48 >= jnp.where(first[1], 8, 7)) & (r48 < jnp.where(last[1], 40, 41))
             & ((l256 < jnp.where(last[2], 128, 129)) | (l256 > jnp.where(first[2], 255, 254))))

    def res0(x, _):
        _, r = residual0(V, x)
        inside = ((x > 1) | jnp.logical_not(first[0])) & ((x < 18) | jnp.logical_not(last[0]))
        st(D, x, jnp.where(keep0 & inside, r, 0.0))
        return 0

    loop(1, 19, res0, 0, chunks=2)

    def rest0(i, _):
        x = 2 + 2 * i
        v = 0.125 * (ld(D, x - 1) + ld(D, x + 2)) + 0.375 * (ld(D, x) + ld(D, x + 1))
        st(RX, i, v)
        for h in (0, 1):
            rows = [RX[h, i, pl.ds(7 + k, 16, stride=2), :] for k in range(4)]
            RX[h, i, 0:16, :] = 0.125 * (rows[0] + rows[3]) + 0.375 * (rows[1] + rows[2])
        return 0

    loop(0, 8, rest0, 0)
    zin = jnp.where(li < 192, li, li - 256)
    wr = restrict_weights(zin, lo - 32, (lo >= 32) & (lo < 96))
    lhs = jnp.concatenate([RX[h, :, 0:16, :].reshape(128, 128) for h in (0, 1)], axis=1)
    B1[6:14, 8:24, :] = dot(lhs, wr).reshape(8, 16, 128)
    ZB[...] = pack_mid(lambda x: B1[6 + x, 8:24, :], 32)
    b_sent = start(
        mid_msgs({1: (9, 1, 5), -1: (6, 14, 5), 0: (6, 6, 8)},
                 lambda xs, ys: B1.at[xs, ys],
                 lambda side, ys: ZB.at[ys], lambda side, j, ys: LB.at[side, j, ys]), 6)

    k2_sent = start(far_msgs(
        lambda d: K2P.at[pl.ds(0, nk(d))] if d[2] == 0 else K2Z.at[(1 - d[2]) // 2],
        lambda d, g, j, ys: LK2.at[g, pl.ds(0, nk(d)), ys] if d[2] == 0 else LK2Z.at[g, j // 2, :, ys]), 8)

    finish(k_sent)
    lane32r = iota((32, 128), 1)

    def z_halo(lm, lp, own, q):
        low = pltpu.roll(lm, 24 + 128 - 16 * q, 1)
        high = pltpu.roll(lp, 88 + 128 - 16 * q, 1)
        return jnp.where(lane32r < 32, low, jnp.where(lane32r < 96, own, high))

    MID = ((0, 0, 6, 2), (1, 6, 8, 0), (2, 14, 5, 0))
    for j, x0, n, i0 in MID:
        def spread_k(i, _, j=j, x0=x0, i0=i0):
            for f in range(4):
                own = pltpu.roll(KP[f // 2, x0 + i], 32 if f % 2 == 0 else 96, 1)
                at = 8 * (i + i0) + 64 * (f % 2)
                low, high = shift(LK[0, j, f // 2], 24 - at, 1), shift(LK[1, j, f // 2], 96 - at, 1)
                K1[f, x0 + i] = jnp.where(lane32r < 32, low, jnp.where(lane32r < 96, own, high))
            return 0

        loop(0, n, spread_k, 0)

    def diag1(x, _):
        fy, fz = K1[1, x], K1[2, x]
        diag = (K1[3, x] + K1[0, x] + K1[0, x - 1]) + (fy + shift(fy, 1, 0)) + (fz + shift(fz, 1, 1))
        I1[x] = 1.0 / diag
        return 0

    loop(1, 19, diag1, 0)

    finish(b_sent)
    for j, x0, n, i0 in ((0, 1, 5, 3), (1, 6, 8, 0), (2, 14, 5, 0)):
        def spread_b(i, _, j=j, x0=x0, i0=i0):
            b = z_halo(LB[0, j], LB[1, j], B1[x0 + i], i + i0)
            B1[x0 + i] = b
            D1[x0 + i] = t_inv * I1[x0 + i] * b
            return 0

        loop(0, n, spread_b, 0)

    def residual(K, ref, b, x, xp, xm, low_y=None):
        v = ref[x]
        fy, fz = K[1, x], K[2, x]
        gz_ = fz * (v - shift(v, -1, 1))
        av = K[3, x] * v + K[0, x] * (v - ref[xp]) + K[0, xm] * (v - ref[xm])
        if low_y is None:
            gy_ = fy * (v - shift(v, -1, 0))
            av = av + (gy_ - shift(gy_, 1, 0))
        else:
            av = av + fy * (v - shift(v, -1, 0)) + low_y * (v - shift(v, 1, 0))
        av = av + (gz_ - shift(gz_, 1, 1))
        return v, b[x] - av

    def pre1(x, _):
        d, r = residual(K1, D1, B1, x, x + 1, x - 1)
        X1[x] = d + (ca * d + cb * I1[x] * r)
        return 0

    loop(2, 18, pre1, 0)

    r32 = iota((32, 128), 0)
    keep1 = ((r32 >= jnp.where(first[1], 8, 7)) & (r32 < jnp.where(last[1], 24, 25))
             & (lane32r >= jnp.where(first[2], 32, 31)) & (lane32r < jnp.where(last[2], 96, 97)))

    def res1(x, _):
        _, r = residual(K1, X1, B1, x, x + 1, x - 1)
        inside = ((x > 5) | jnp.logical_not(first[0])) & ((x < 14) | jnp.logical_not(last[0]))
        D1[x] = jnp.where(keep1 & inside, r, 0.0)
        return 0

    loop(5, 15, res1, 0)

    rows = []
    for i in range(4):
        x = 6 + 2 * i
        RX1[i] = 0.125 * (D1[x - 1] + D1[x + 2]) + 0.375 * (D1[x] + D1[x + 1])
        parts = [RX1[i, pl.ds(7 + k, 8, stride=2), :] for k in range(4)]
        rows.append(0.125 * (parts[0] + parts[3]) + 0.375 * (parts[1] + parts[2]))
    B2P[...] = packed(jnp.concatenate(rows, 0), restrict_weights(wi - 32, wo, in32))
    b2_sent = start(far_msgs(lambda d: B2P, lambda d, g, j, ys: LB2.at[g, j, ys]), 10)
    LB2[gx, 1, 8:16, :] = B2P[...]

    NX2 = 4 * GX
    finish(k2_sent)
    lane24 = iota((24, 128), 1)

    def unpack2(lm, lc, lp, i):
        return jnp.where(lane24 < 32, pltpu.roll(lm, 128 - 32 * i, 1),
                         jnp.where(lane24 < 64, pltpu.roll(lc, 160 - 32 * i, 1), pltpu.roll(lp, 192 - 32 * i, 1)))

    def spread_k2(x, _):
        g, i = x >> 2, x & 3
        k2 = []
        for f in range(5):
            t, at = spot(f, i)
            low, high = shift(LK2Z[g, 0, t], 20 - at, 1), shift(LK2Z[g, 1, t], 64 - at, 1)
            own = shift(LK2[g, f], 32 - 32 * i, 1)
            k2.append(jnp.where(lane24 < 32, low, jnp.where(lane24 < 64, own, high)))
        for f in range(4):
            K2[f, x] = k2[f]
        K2[4, x] = jnp.where(iota((24, 128), 0) < 8, k2[4], shift(k2[1], 1, 0))
        return 0

    loop(0, NX2, spread_k2, 0)

    def up(x):
        return lax.rem(x + 1, NX2)

    def down(x):
        return lax.rem(x + (NX2 - 1), NX2)

    def diag2(x, _):
        fz = K2[2, x]
        diag = (K2[3, x] + K2[0, x] + K2[0, down(x)]) + (K2[1, x] + K2[4, x]) + (fz + shift(fz, 1, 1))
        I2[x] = 1.0 / diag
        return 0

    loop(0, NX2, diag2, 0)

    t2_inv, factors2 = cheb_factors(6, 0.05, 2.0)
    finish(b2_sent)

    def spread_b2(x, _):
        g, i = x >> 2, x & 3
        b = unpack2(LB2[g, 0], LB2[g, 1], LB2[g, 2], i)
        Y2[x] = b
        d = t2_inv * I2[x] * b
        D2[x] = d
        X2[0, x] = d
        return 0

    loop(0, NX2, spread_b2, 0)

    r24 = iota((24, 128), 0)
    keep2 = ((r24 >= jnp.where(first[1], 8, 4)) & (r24 < jnp.where(last[1], 16, 20))
             & (lane24 >= jnp.where(first[2], 32, 28)) & (lane24 < jnp.where(last[2], 64, 68)))
    for n, (fa, fb) in enumerate(factors2):
        src, dst = X2.at[n % 2], X2.at[1 - n % 2]
        final = n == len(factors2) - 1

        def step(x, _, src=src, dst=dst, fa=fa, fb=fb, final=final):
            v, r = residual(K2, src, Y2, x, up(x), down(x), K2[4, x])
            d = fa * D2[x] + fb * I2[x] * r
            if final:
                dst[x] = jnp.where(keep2, v + d, 0.0)
            else:
                D2[x] = d
                dst[x] = v + d
            return 0

        loop(0, NX2, step, 0)
    x2 = X2.at[len(factors2) % 2]

    wp = prolong_weights(wi - 32, wo - 32)
    z1 = dot(x2[...].reshape(NX2 * 24, 128), wp).reshape(NX2, 24, 128)
    Y2[...] = z1

    def pro_y1(x, _):
        c = Y2[x]
        lower, upper = shift(c, 1, 0), shift(c, -1, 0)
        PY1[x, pl.ds(0, 16, stride=2), :] = (0.75 * c + 0.25 * lower)[4:20]
        PY1[x, pl.ds(1, 16, stride=2), :] = (0.75 * c + 0.25 * upper)[4:20]
        return 0

    loop(0, NX2, pro_y1, 0)

    def pro_x1(i, _):
        a = 4 * gx + (i - 3)

        def slab(k):
            return jnp.where((k >= 0) & (k < NX2), PY1[lax.rem(k + NX2, NX2)], 0.0)

        c = 0.75 * slab(a)
        X1[2 * i] = X1[2 * i] + (c + 0.25 * slab(a - 1))
        X1[2 * i + 1] = X1[2 * i + 1] + (c + 0.25 * slab(a + 1))
        return 0

    loop(1, 9, pro_x1, 0)

    def post1(x, _):
        v, r = residual(K1, X1, B1, x, x + 1, x - 1)
        d = t_inv * I1[x] * r
        D1[x] = d
        T1[x] = v + d
        return 0

    loop(3, 17, post1, 0)
    keep1p = ((r32 >= jnp.where(first[1], 8, 4)) & (r32 < jnp.where(last[1], 24, 28))
              & (lane32r >= jnp.where(first[2], 32, 28)) & (lane32r < jnp.where(last[2], 96, 100)))

    def post1b(x, _):
        v, r = residual(K1, T1, B1, x, x + 1, x - 1)
        inside = ((x > 5) | jnp.logical_not(first[0])) & ((x < 14) | jnp.logical_not(last[0]))
        X1[x] = jnp.where(keep1p & inside, v + (ca * D1[x] + cb * I1[x] * r), 0.0)
        return 0

    loop(4, 16, post1b, 0)

    pi, po = iota((128, 256), 0), iota((128, 256), 1)
    wq = prolong_weights(pi - 32, jnp.where(po < 192, po, po - 256))
    for i in range(12):
        z0 = dot(X1[4 + i], wq)
        lower, upper = shift(z0, 1, 0), shift(z0, -1, 0)
        ev, od = 0.75 * z0 + 0.25 * lower, 0.75 * z0 + 0.25 * upper
        for h in (0, 1):
            PY0[h, i, pl.ds(0, 24, stride=2), :] = ev[4:28, 128 * h:128 * h + 128]
            PY0[h, i, pl.ds(1, 24, stride=2), :] = od[4:28, 128 * h:128 * h + 128]

    def pro_x0(i, _):
        c = 0.75 * ld(PY0, i + 1)
        st(V, 2 * i, ld(V, 2 * i) + (c + 0.25 * ld(PY0, i)))
        st(V, 2 * i + 1, ld(V, 2 * i + 1) + (c + 0.25 * ld(PY0, i + 2)))
        return 0

    loop(0, 10, pro_x0, 0)

    def post0(x, _):
        v, r = residual0(V, x)
        d = t_inv * ld(ID, x) * r
        st(D, x, d)
        st(W, x, v + d)
        return 0

    loop(1, 19, post0, 0, chunks=2)

    def post0b(x, _):
        v, r = own_residual0(W, x)
        out[x - 2] = v + (ca * D[0, x, 8:40, :] + cb * ID[0, x, 8:40, :] * r)
        return 0

    loop(2, 18, post0b, 0, chunks=2)


def solution(mesh):
    sizes = tuple(mesh.shape[a] for a in ("gx", "gy", "gz"))
    nx2 = 4 * sizes[0]

    def vm(*shape):
        return pltpu.VMEM(shape, F32)

    dma = lambda n: pltpu.SemaphoreType.DMA((n,))
    scratch = [
        vm(5, 2, 20, 48, 128), vm(2, 20, 48, 128), vm(2, 20, 48, 128), vm(2, 20, 48, 128), vm(2, 20, 48, 128),
        vm(2, 8, 48, 128), vm(3, 32, 128), vm(2, 5, 48, 128), vm(1, 32, 128), vm(2, 3, 48, 128),
        vm(2, 20, 32, 128), vm(4, 20, 32, 128), vm(2, 2, 16, 128), vm(2, 3, 2, 32, 128),
        vm(20, 32, 128), vm(20, 32, 128), vm(20, 32, 128), vm(20, 32, 128), vm(20, 32, 128),
        vm(16, 128), vm(2, 3, 32, 128), vm(4, 32, 128),
        vm(5, 8, 128), vm(sizes[0], 5, 24, 128), vm(2, 2, 8, 128), vm(sizes[0], 2, 2, 24, 128),
        vm(8, 128), vm(sizes[0], 3, 24, 128),
        vm(5, nx2, 24, 128), vm(nx2, 24, 128), vm(2, nx2, 24, 128), vm(nx2, 24, 128), vm(nx2, 24, 128),
        vm(nx2, 32, 128), vm(2, 12, 48, 128),
        vm(2, 6, 16, 128), vm(2, 6, 16, 128), vm(4, 8, 128), vm(4, 8, 128),
        vm(2, 2, 16, 128), vm(2, 2, 16, 128), vm(4, 8, 128), vm(4, 8, 128),
        vm(512, 8, 128), dma(5), dma(12),
    ]

    def local(right_side, face_x, face_y, face_z, absorb):
        return pl.pallas_call(
            functools.partial(kernel, sizes),
            out_shape=jax.ShapeDtypeStruct(right_side.shape, F32),
            in_specs=[pl.BlockSpec(memory_space=pltpu.HBM)] * 5,
            out_specs=pl.BlockSpec(memory_space=pltpu.VMEM),
            scratch_shapes=scratch,
            compiler_params=pltpu.CompilerParams(
                collective_id=0, has_side_effects=True, vmem_limit_bytes=62 * 1024 * 1024),
            name="vcycle",
        )(right_side, face_x, face_y, face_z, absorb)

    spec = P("gx", "gy", "gz")
    return jax.shard_map(local, mesh=mesh, in_specs=(spec,) * 5, out_specs=spec, check_vma=False)
```
